128 devices in a mesh: gx: 16 (over y, x), gy: 8 (over z, core).
Axes of the slice: x: 4, y: 4, z: 4, core: 2. Of those that a mesh axis runs over, the one named last changes fastest.
Arguments:
- features: bfloat16 [128, 128, 2048], P('gx', 'gy'), may hold values from -6 to 6
- labels: int32 [128, 128, 32], P('gx', 'gy'), may hold values from 0 to 255
- lists: int32 [128, 256], P(('gx', 'gy')), may hold values from 0 to 8191, as said below
- home: int32 [8192], replicated, may hold values from 0 to 8191, as said below
- conv_first: bfloat16 [1728, 64], replicated, may hold values from -0.15625 to 0.15625
- conv_second: bfloat16 [1728, 64], replicated, may hold values from -0.15625 to 0.15625
- head_in: bfloat16 [64, 256], replicated, may hold values from -12 to 12
- head_out: bfloat16 [256, 128], replicated, may hold values from -0.375 to 0.375
Outputs:
- embeddings: bfloat16 [8192, 128], P(('gx', 'gy'))
The draws below stay inside these ranges and needn't reach their ends.
Inputs may be any that keep to these rules, and one draw needn't show every extreme that they name: `lists`: entries of a row are distinct. Of one row's labels, at most 8 have segments whose home rows lie in one block of 64 rows, and that many is reached in every row. `home`: A permutation of the segments.
All inputs are finite; a program needn't handle non-finite values.
Results may differ from the reference program's by a relative error of at most 0.015.
Values may be sent and summed in bfloat16 or wider, within the bound.
No kernel may reach another device: no remote copies, remote signals or barrier semaphores. Data moves between devices by JAX's collectives and lax.ppermute only.
A program may use at most 128 MiB of HBM per device.

```python
import jax
import jax.numpy as jnp
from jax import lax

C = 64
HID = 256
E = 128
CX = 8
CY = 16
Z = 32
L = 256
CAP = 8
SEG_DEV = 64
NX = 128
NY = 128
SEGS = 8192
N_GY = 8
DEVICES = 128


def shared_order(key):
    return jax.random.permutation(jax.random.fold_in(key, 11), SEGS).astype(jnp.int32)


def draw_home(key, part):
    seg_order = shared_order(key)
    return seg_order


def draw_lists(key, part):
    seg_order = shared_order(key)
    key = jax.random.fold_in(key, 3)
    inverse = jnp.argsort(seg_order).astype(jnp.int32)
    hot_key, dev_key = jax.random.split(key)
    ranking = jax.random.permutation(hot_key, DEVICES).astype(jnp.int32)
    hot_count = L // (2 * CAP)
    half_slots = L // 2

    def one_device(dev_index):
        key_pool, key_offset, key_order = jax.random.split(jax.random.fold_in(dev_key, dev_index), 3)
        first_half = jnp.arange(half_slots, dtype=jnp.int32)
        spare_pool = jax.random.permutation(key_pool, (DEVICES - hot_count) * CAP)[:half_slots].astype(jnp.int32)
        owner_dev = jnp.concatenate([ranking[first_half // CAP], ranking[hot_count + spare_pool // CAP]])
        slot_rank = jnp.concatenate([first_half % CAP, spare_pool % CAP])
        offsets = jax.random.randint(key_offset, (DEVICES,), 0, SEG_DEV).astype(jnp.int32)
        home_row = owner_dev * SEG_DEV + (offsets[owner_dev] + slot_rank) % SEG_DEV
        segment = inverse[home_row]
        return segment[jax.random.permutation(key_order, L)]
    return jax.vmap(one_device)(jnp.arange(DEVICES, dtype=jnp.int32)).astype(jnp.int32)


def plant(drawn, rng, least, largest):
    place = [jax.random.randint(jax.random.fold_in(rng, axis), (), 0, length) for axis, length in enumerate(drawn.shape)]
    main_axis = drawn.shape.index(max(drawn.shape))
    beside = place[:main_axis] + [(place[main_axis] + 1) % drawn.shape[main_axis]] + place[main_axis + 1:]
    return drawn.at[tuple(place)].set(least).at[tuple(beside)].set(largest)


def steps_of(stream_key, extent, pieces, low, top_value):
    factor_of = 1.0
    for position, parts in pieces:
        steps = jax.random.uniform(jax.random.fold_in(jax.random.fold_in(stream_key, 6), position), (parts,), jnp.float32, low / len(pieces), top_value / len(pieces))
        factor_of = factor_of * jnp.repeat(jnp.exp(steps), extent[position] // parts).reshape((-1,) + (1,) * (len(extent) - 1 - position))
    return factor_of


def bell_draw(key, shape, deviation, limit, pieces=(), kind=jnp.bfloat16):
    entries = deviation * jax.random.normal(key, shape, jnp.float32)
    if pieces:
        entries = entries * steps_of(key, shape, pieces, -0.22, 0.18)
    return jnp.clip(entries, -limit, limit).astype(kind)


def setup_inputs(seed: int = 0) -> dict:
    keys = jax.random.split(jax.random.key(seed), 9)
    return {
        "features": bell_draw(keys[0], (NX, NY, Z * C), 1.0, 6.0, ((0, 16), (1, 8))),
        "labels": plant(jax.random.randint(keys[1], (NX, NY, Z), 0, L), jax.random.fold_in(keys[1], 1), 0, L - 1).astype(jnp.int32),
        "lists": draw_lists(jax.random.fold_in(keys[8], 71), 0),
        "home": draw_home(jax.random.fold_in(keys[8], 71), 0),
        "conv_first": bell_draw(keys[4], (27 * C, C), (27 * C) ** -0.5, 0.15625),
        "conv_second": bell_draw(keys[5], (27 * C, C), (27 * C) ** -0.5, 0.15625),
        "head_in": bell_draw(keys[6], (C, HID), 2.0, 12.0),
        "head_out": bell_draw(keys[7], (HID, E), HID ** -0.5, 0.375),
    }


def residual_layer(volume, weight):
    kernel = weight.reshape(3, 3, 3, C, C).astype(jnp.float32)
    active = jnp.maximum(volume, 0).astype(jnp.float32)[None]
    branch = lax.conv_general_dilated(active, kernel, (1, 1, 1), "SAME", dimension_numbers=("NDHWC", "DHWIO", "NDHWC"), precision=lax.Precision.HIGHEST)[0]
    return (volume.astype(jnp.float32) + branch).astype(jnp.bfloat16)


def reference(features, labels, lists, home, conv_first, conv_second, head_in, head_out):
    volume = features.reshape(NX, NY, Z, C)
    first = residual_layer(volume, conv_first)
    second = residual_layer(first, conv_second)
    tile_x = (jnp.arange(NX) // CX).astype(jnp.int32)
    tile_y = (jnp.arange(NY) // CY).astype(jnp.int32)
    dev_index = tile_x[:, None] * N_GY + tile_y[None, :]
    segment = lists[dev_index[:, :, None], labels]
    home_row = home[segment].reshape(-1)
    flat = second.reshape(NX * NY * Z, C).astype(jnp.float32)
    sums = jax.ops.segment_sum(flat, home_row, num_segments=SEGS)
    counts = jax.ops.segment_sum(jnp.ones((NX * NY * Z,), jnp.float32), home_row, num_segments=SEGS)
    means = sums / jnp.maximum(counts, 1.0)[:, None]
    hidden = jnp.maximum(jnp.dot(means.astype(jnp.bfloat16), head_in, preferred_element_type=jnp.float32), 0.0).astype(jnp.bfloat16)
    return jnp.dot(hidden, head_out, preferred_element_type=jnp.float32).astype(jnp.bfloat16)
```

```python
import functools

import jax
import jax.numpy as jnp
from jax import lax
from jax.experimental import pallas as pl
from jax.experimental.pallas import tpu as pltpu
from jax.sharding import PartitionSpec as P

F32 = jnp.float32
BF16 = jnp.bfloat16
SX, SY, SZ, CH = 8, 16, 32, 64
LANES = SZ * CH
WIDE = LANES + 2 * CH
NB = 8
EX = SX + 4
FX = SX + 2
CAP = 8
VMEM = pl.BlockSpec(memory_space=pltpu.VMEM)
SMEM = pl.BlockSpec(memory_space=pltpu.SMEM)


def params(mb=40):
    return pltpu.CompilerParams(vmem_limit_bytes=mb * 2**20)


def iota(shape, dim):
    return lax.broadcasted_iota(jnp.int32, shape, dim)


def dot(a, b):
    return jnp.dot(a, b, preferred_element_type=F32)


def widen(rows):
    zero = jnp.zeros((rows.shape[0], CH), rows.dtype)
    return jnp.concatenate([zero, rows, zero], axis=1)


def relu(rows):
    return jnp.maximum(rows, jnp.zeros_like(rows))


def band(w_ref, out_ref):
    zero = jnp.zeros((CH, CH), BF16)
    quiet = jnp.zeros((128, 128), BF16)
    for kx in range(3):
        for ky in range(3):
            start = (kx * 3 + ky) * 3 * CH
            w = w_ref[start : start + 3 * CH, :]
            both = jnp.concatenate(
                [jnp.concatenate([w, zero], axis=0), jnp.concatenate([zero, w], axis=0)], axis=1
            )
            base = kx * 384
            out_ref[ky, base : base + 256, 0:128] = both
            out_ref[ky, base + 128 : base + 384, 128:256] = both
            out_ref[ky, base + 256 : base + 384, 0:128] = quiet
            out_ref[ky, base : base + 128, 128:256] = quiet


def prepare_kernel(labels, lists, home, w1, w2, wb1, wb2, member, place, meta):
    slots = lists.shape[1]
    devices = home.shape[0]
    band(w1, wb1)
    band(w2, wb2)
    lab = labels[...].reshape(SX * SY, SZ).T
    ids = iota((slots, SX * SY), 0)
    count = jnp.zeros((slots, SX * SY), F32)
    for z in range(SZ):
        hit = jnp.broadcast_to(lab[z : z + 1, :], (slots, SX * SY)) == ids
        hot = hit.astype(F32)
        count = count + hot
        j, b = z % 4, z // 4
        member[j * slots : (j + 1) * slots, b * 128 : (b + 1) * 128] = hot.astype(BF16)
    count = jnp.sum(count, axis=1, keepdims=True)
    li = lists[...]
    rows = home.shape[0]
    which = (iota((rows, slots), 0) == jnp.broadcast_to(li >> 7, (rows, slots))).astype(BF16)
    table = home[...]
    high = (table >> 6).astype(F32).T.astype(BF16)
    low = (table & 63).astype(F32).T.astype(BF16)
    lane = iota((128, slots), 0) == jnp.broadcast_to(li & 127, (128, slots))
    owner = jnp.sum(jnp.where(lane, dot(high, which), 0.0), axis=0, keepdims=True)
    row = jnp.sum(jnp.where(lane, dot(low, which), 0.0), axis=0, keepdims=True)
    across = jnp.broadcast_to(owner, (slots, slots))
    same = (across.T == across) & (iota((slots, slots), 0) < iota((slots, slots), 1))
    rank = jnp.sum(same.astype(F32), axis=0, keepdims=True)
    at = (owner * CAP + rank).astype(jnp.int32)
    total = place.shape[0]
    place[...] = (iota((total, slots), 0) == jnp.broadcast_to(at, (total, slots))).astype(F32).astype(BF16)
    key = jnp.broadcast_to(row + 1.0, (128, slots)).T
    count = jnp.broadcast_to(count, (slots, 128))
    big = jnp.floor(count * (1.0 / 64.0))
    lanes = iota((slots, 128), 1)
    info = jnp.where(lanes == 64, key, 0.0)
    info = jnp.where(lanes == 65, big, info)
    info = jnp.where(lanes == 66, count - 64.0 * big, info)
    meta[...] = info.astype(BF16)


def prepare(labels, lists, home, w1, w2, devices):
    slots = lists.shape[1]
    return pl.pallas_call(
        prepare_kernel,
        out_shape=(
            jax.ShapeDtypeStruct((3, 1152, 256), BF16),
            jax.ShapeDtypeStruct((3, 1152, 256), BF16),
            jax.ShapeDtypeStruct((4 * slots, NB * SX * SY), BF16),
            jax.ShapeDtypeStruct((devices * CAP, slots), BF16),
            jax.ShapeDtypeStruct((slots, 128), BF16),
        ),
        in_specs=[VMEM] * 5,
        out_specs=(VMEM,) * 5,
        compiler_params=params(),
        cost_estimate=pl.CostEstimate(flops=10**8, bytes_accessed=8 * 2**20, transcendentals=0),
        name="prepare",
    )(labels, lists, home, w1, w2)


def choose(flag, yes, no):
    return jnp.where(flag, yes.astype(F32), no.astype(F32)).astype(BF16)


def x_extended(even, v, xa, xb):
    a = xa[...]
    b = xb[...]
    low = choose(even, b, a)
    high = choose(even, a, b)
    return jnp.concatenate([low, v[...], high], axis=0)


def columns_kernel(where, v, xa, xb, near, far):
    x_even = where[0] % 2 == 0
    y_even = where[1] % 2 == 0
    block = x_extended(x_even, v, xa, xb).reshape(EX * SY, LANES)
    r = iota((64, EX * SY), 0)
    c = r // 16
    y = jnp.where(c < 2, c, c + 12)
    pick = ((r % 16) * 16 + y == iota((64, EX * SY), 1)).astype(F32).astype(BF16)
    cols = dot(pick, block).astype(BF16)

    @pl.when(y_even)
    def _():
        near[...] = cols[32:64]
        far[...] = cols[0:32]

    @pl.when(jnp.logical_not(y_even))
    def _():
        near[...] = cols[0:32]
        far[...] = cols[32:64]


def columns(where, v, xa, xb):
    shape = jax.ShapeDtypeStruct((32, LANES), BF16)
    return pl.pallas_call(
        columns_kernel,
        out_shape=(shape, shape),
        in_specs=[SMEM, VMEM, VMEM, VMEM],
        out_specs=(VMEM, VMEM),
        compiler_params=params(),
        name="columns",
    )(where, v, xa, xb)


def windows(wide_ref, rows_out, pitch):
    parts = []
    for b in range(NB):
        parts.append(
            jnp.concatenate(
                [
                    wide_ref[kx * pitch : kx * pitch + rows_out, 256 * b : 256 * b + 384]
                    for kx in range(3)
                ],
                axis=1,
            )
        )
    return jnp.concatenate(parts, axis=0)


def blocks(rows):
    return jnp.concatenate([rows[:, 256 * b : 256 * b + 256] for b in range(NB)], axis=0)


def unblocks(stack):
    n = stack.shape[0] // NB
    return jnp.concatenate([stack[n * b : n * b + n] for b in range(NB)], axis=1)


def fold_y(below, same, above):
    n = same.shape[0]
    y = iota((n, 256), 0) % SY
    down = jnp.where(y == 0, 0.0, pltpu.roll(below, 1, 0))
    up = jnp.where(y == SY - 1, 0.0, pltpu.roll(above, n - 1, 0))
    return same + down + up


def inner_kernel(where, v, xa, xb, wb, out, wide):
    x_even = where[0] % 2 == 0
    block = x_extended(x_even, v, xa, xb).reshape(EX * SY, LANES)
    wide[...] = widen(relu(block))
    left = windows(wide, FX * SY, SY)
    conv = fold_y(dot(left, wb[0]), dot(left, wb[1]), dot(left, wb[2]))
    out[...] = conv + blocks(block[SY : SY + FX * SY]).astype(F32)


def inner(where, v, xa, xb, wb):
    return pl.pallas_call(
        inner_kernel,
        out_shape=jax.ShapeDtypeStruct((NB * FX * SY, 256), F32),
        in_specs=[SMEM, VMEM, VMEM, VMEM, VMEM],
        out_specs=VMEM,
        scratch_shapes=[pltpu.VMEM((EX * SY, WIDE), BF16)],
        compiler_params=params(),
        cost_estimate=pl.CostEstimate(flops=4 * 10**9, bytes_accessed=2 * 2**20, transcendentals=0),
        name="inner",
    )(where, v, xa, xb, wb)


def rolled(cols, kx):
    return cols if kx == 0 else pltpu.roll(cols, cols.shape[0] - kx, 0)


def spread(edge, count):
    return jnp.concatenate(
        [
            jnp.broadcast_to(edge[16 * b + x : 16 * b + x + 1, :], (SY, 256))
            for b in range(NB)
            for x in range(count)
        ],
        axis=0,
    )


def outer_kernel(
    where, part, near, far, ya, yb, wb1, wb2, member, place, meta, out, cols1, wide2, cols2
):
    gx, gy = where[0], where[1]
    last_x, last_y = where[2] - 1, where[3] - 1
    y_even = gy % 2 == 0
    own_low = choose(y_even, far[...], near[...])[0:16]
    own_high = choose(y_even, near[...], far[...])[16:32]
    low = choose(y_even, yb[...], ya[...])
    high = choose(y_even, ya[...], yb[...])
    edge = jnp.concatenate(
        [low[0:16], own_high, low[16:32], high[0:16], high[16:32], own_low], axis=0
    ).astype(F32)
    active = relu(edge)
    for kx in range(3):
        cols1[kx] = widen(rolled(active, kx).astype(BF16))

    def left(first, count):
        parts = []
        for b in range(NB):
            parts.append(
                jnp.concatenate(
                    [
                        cols1[kx, 16 * first : 16 * (first + count), 256 * b : 256 * b + 384]
                        for kx in range(3)
                    ],
                    axis=1,
                )
            )
        return jnp.concatenate(parts, axis=0)

    z0 = dot(left(0, 3), wb1[0]).reshape(NB, 48, 256)
    z1 = dot(left(2, 2), wb1[1]).reshape(NB, 32, 256)
    z2 = dot(left(3, 3), wb1[2]).reshape(NB, 48, 256)
    residual = rolled(edge, 1)
    x = iota((NB * 16, 256), 0) % 16 - 1
    inside = (x >= jnp.where(gx == 0, 0, -1)) & (x <= jnp.where(gx == last_x, SX - 1, SX))
    low_first = (
        (z0[:, 0:16] + z1[:, 0:16] + z2[:, 32:48]).reshape(NB * 16, 256) + blocks(residual[32:48])
    )
    high_first = (
        (z0[:, 16:32] + z1[:, 16:32] + z2[:, 16:32]).reshape(NB * 16, 256) + blocks(residual[48:64])
    )
    low_first = jnp.where(inside & (gy > 0), low_first, 0.0)
    high_first = jnp.where(inside & (gy < last_y), high_first, 0.0)
    from_low = z0[:, 32:48].reshape(NB * 16, 256)
    from_high = z2[:, 0:16].reshape(NB * 16, 256)

    n = NB * FX * SY
    row = iota((n, 256), 0)
    y = row % SY
    x = (row // SY) % FX - 1
    first = part[...]
    first = first + jnp.where(y == 0, spread(from_low, FX), 0.0)
    first = first + jnp.where(y == SY - 1, spread(from_high, FX), 0.0)
    inside = (x >= jnp.where(gx == 0, 0, -1)) & (x <= jnp.where(gx == last_x, SX - 1, SX))
    first = jnp.where(inside, first, 0.0).astype(BF16)
    wide2[...] = widen(relu(unblocks(first)))
    sides = relu(
        jnp.concatenate([unblocks(low_first), unblocks(high_first)], axis=0).astype(BF16)
    ).astype(F32)
    for kx in range(3):
        cols2[kx] = widen(rolled(sides, kx).astype(BF16))
    w0, w1, w2 = wb2[0], wb2[1], wb2[2]

    def side(first):
        parts = []
        for b in range(NB):
            parts.append(
                jnp.concatenate(
                    [cols2[kx, first : first + 16, 256 * b : 256 * b + 384] for kx in range(3)],
                    axis=1,
                )
            )
        return jnp.concatenate(parts, axis=0)

    left2 = windows(wide2, SX * SY, SY)
    conv = fold_y(dot(left2, w0), dot(left2, w1), dot(left2, w2))
    y = iota((NB * SX * SY, 256), 0) % SY
    conv = conv + jnp.where(y == 0, spread(dot(side(0), w0), SX), 0.0)
    conv = conv + jnp.where(y == SY - 1, spread(dot(side(16), w2), SX), 0.0)
    own = jnp.concatenate(
        [first[FX * SY * b + SY : FX * SY * b + SY + SX * SY] for b in range(NB)], axis=0
    )
    second = (own.astype(F32) + conv).astype(BF16)
    slots = meta.shape[0]
    a = dot(member[0 : 2 * slots, :], second[:, 0:128])
    c = dot(member[2 * slots : 4 * slots, :], second[:, 128:256])
    a = a + c
    lanes = iota((slots, 128), 1)
    sums = a[0:slots] + pltpu.roll(a[slots : 2 * slots], 64, 1)
    rows = jnp.where(lanes < CH, sums, meta[...].astype(F32)).astype(BF16)
    out[...] = dot(place[...], rows).astype(BF16)


def outer(where, part, near, far, ya, yb, wb1, wb2, member, place, meta):
    return pl.pallas_call(
        outer_kernel,
        out_shape=jax.ShapeDtypeStruct((place.shape[0], 128), BF16),
        in_specs=[SMEM] + [VMEM] * 10,
        out_specs=VMEM,
        scratch_shapes=[
            pltpu.VMEM((3, 96, WIDE), BF16),
            pltpu.VMEM((FX * SY, WIDE), BF16),
            pltpu.VMEM((3, 32, WIDE), BF16),
        ],
        compiler_params=params(),
        name="outer",
    )(where, part, near, far, ya, yb, wb1, wb2, member, place, meta)


def head_kernel(got, w_in, w_out, out):
    rows = got[...]
    n = rows.shape[0]
    seg = out.shape[0]
    unit = (iota((8, 128), 1) == CH).astype(F32).astype(BF16)
    key = lax.dot_general(unit, rows, (((1,), (1,)), ((), ())), preferred_element_type=F32)
    key = jnp.broadcast_to(key[0:1], (seg, n))
    hit = (key == (iota((seg, n), 0) + 1).astype(F32)).astype(F32).astype(BF16)
    total = dot(hit, rows)
    lanes = iota((seg, 128), 1)
    digits = jnp.where(lanes == CH + 1, total * 64.0, jnp.where(lanes == CH + 2, total, 0.0))
    count = jnp.sum(digits, axis=1, keepdims=True)
    means = (total[:, 0:CH] / jnp.maximum(count, 1.0)).astype(BF16)
    hidden = jnp.maximum(dot(means, w_in[...]), 0.0).astype(BF16)
    out[...] = dot(hidden, w_out[...]).astype(BF16)


def head(got, w_in, w_out, seg):
    return pl.pallas_call(
        head_kernel,
        out_shape=jax.ShapeDtypeStruct((seg, w_out.shape[1]), BF16),
        in_specs=[VMEM] * 3,
        out_specs=VMEM,
        compiler_params=params(),
        name="head",
    )(got, w_in, w_out)


def pairs(count):
    inner_pairs = [(i, i ^ 1) for i in range(count)]
    outer_pairs = [(i, i + 1 if i % 2 else i - 1) for i in range(1, count - 1)]
    return inner_pairs, outer_pairs


def local(n_gx, n_gy, features, labels, lists, home, conv_first, conv_second, head_in, head_out):
    gx = lax.axis_index("gx")
    gy = lax.axis_index("gy")
    devices = n_gx * n_gy
    where = jnp.stack([gx, gy, jnp.int32(n_gx), jnp.int32(n_gy)]).astype(jnp.int32)
    even = gx % 2 == 0
    to_a = lax.dynamic_slice_in_dim(features, jnp.where(even, SX - 2, 0), 2, 0)
    to_b = lax.dynamic_slice_in_dim(features, jnp.where(even, 0, SX - 2), 2, 0)
    inner_x, outer_x = pairs(n_gx)
    inner_y, outer_y = pairs(n_gy)
    xa = lax.ppermute(to_a, "gx", inner_x)
    xb = lax.ppermute(to_b, "gx", outer_x)
    wb1, wb2, member, place, meta = prepare(
        labels, lists, home.reshape(-1, 128), conv_first, conv_second, devices
    )
    near, far = columns(where, features, xa, xb)
    ya = lax.ppermute(near, "gy", inner_y)
    yb = lax.ppermute(far, "gy", outer_y)
    part = inner(where, features, xa, xb, wb1)
    rows = outer(where, part, near, far, ya, yb, wb1, wb2, member, place, meta)
    rows = rows.reshape(devices, CAP, 128)
    got = lax.all_to_all(rows, ("gx", "gy"), 0, 0, tiled=True)
    return head(got.reshape(devices * CAP, 128), head_in, head_out, home.shape[0] // devices)


def solution(mesh):
    placed = (
        P("gx", "gy", None),
        P("gx", "gy", None),
        P(("gx", "gy"), None),
        P(),
        P(),
        P(),
        P(),
        P(),
    )
    return jax.shard_map(
        functools.partial(local, mesh.shape["gx"], mesh.shape["gy"]),
        mesh=mesh,
        in_specs=placed,
        out_specs=P(("gx", "gy"), None),
        check_vma=False,
    )
```

```python
import functools

import jax
import jax.numpy as jnp
from jax import lax
from jax.experimental import pallas as pl
from jax.experimental.pallas import tpu as pltpu
from jax.sharding import PartitionSpec as P

F32 = jnp.float32
BF16 = jnp.bfloat16
SX, SY, SZ, CH = 8, 16, 32, 64
LANES = SZ * CH
WIDE = LANES + 2 * CH
NB = 8
EX = SX + 4
FX = SX + 2
CAP = 8
STEP = 8
VMEM = pl.BlockSpec(memory_space=pltpu.VMEM)
SMEM = pl.BlockSpec(memory_space=pltpu.SMEM)


def params(mb=20):
    return pltpu.CompilerParams(vmem_limit_bytes=mb * 2**20)


def iota(shape, dim):
    return lax.broadcasted_iota(jnp.int32, shape, dim)


def dot(a, b):
    return jnp.dot(a, b, preferred_element_type=F32)


def widen(rows):
    zero = jnp.zeros((rows.shape[0], CH), rows.dtype)
    return jnp.concatenate([zero, rows, zero], axis=1)


def relu(rows):
    return jnp.maximum(rows, jnp.zeros_like(rows))


def begin_kernel(out):
    out[...] = jnp.zeros_like(out)


def begin():
    return pl.pallas_call(
        begin_kernel,
        out_shape=jax.ShapeDtypeStruct((8, 128), F32),
        out_specs=VMEM,
        cost_estimate=pl.CostEstimate(flops=10**10, bytes_accessed=4096, transcendentals=0),
        name="begin",
    )()


def band(wt_ref, out_ref):
    weight = wt_ref[...].astype(F32).T.astype(BF16)
    zero = jnp.zeros((CH, CH), BF16)
    quiet = jnp.zeros((128, 128), BF16)
    for kx in range(3):
        for ky in range(3):
            start = (kx * 3 + ky) * 3 * CH
            w = weight[start : start + 3 * CH, :]
            both = jnp.concatenate(
                [jnp.concatenate([w, zero], axis=0), jnp.concatenate([zero, w], axis=0)], axis=1
            )
            base = (ky * 3 + kx) * 384
            out_ref[base : base + 256, 0:128] = both
            out_ref[base + 128 : base + 384, 128:256] = both
            out_ref[base + 256 : base + 384, 0:128] = quiet
            out_ref[base : base + 128, 128:256] = quiet


def blocks(rows):
    return jnp.concatenate([rows[:, 256 * b : 256 * b + 256] for b in range(NB)], axis=0)


def unblocks(stack):
    n = stack.shape[0] // NB
    return jnp.concatenate([stack[n * b : n * b + n] for b in range(NB)], axis=1)


def shifts_y(wide):
    n = wide.shape[0]
    grid = wide.reshape(n // SY, SY, WIDE)
    zero = jnp.zeros((n // SY, 1, WIDE), wide.dtype)
    below = jnp.concatenate([zero, grid[:, : SY - 1]], axis=1).reshape(n, WIDE)
    above = jnp.concatenate([grid[:, 1:], zero], axis=1).reshape(n, WIDE)
    return below, wide, above


def windows(shifted, starts, rows):
    parts = []
    for b in range(NB):
        for start in starts:
            parts.append(
                jnp.concatenate(
                    [
                        ref[start + kx * SY : start + kx * SY + rows, 256 * b : 256 * b + 384]
                        for ref in shifted
                        for kx in range(3)
                    ],
                    axis=1,
                )
            )
    return jnp.concatenate(parts, axis=0)


def before_kernel(begun, v, labels, lists, home, w1t, w2t, wb1, wb2, member, place, meta, core, s0, s1, s2):
    slots = lists.shape[1]
    band(w1t, wb1)
    own = v[...].reshape(SX * SY, LANES)
    s0[...], s1[...], s2[...] = shifts_y(widen(relu(own)))
    conv = dot(windows((s0, s1, s2), (0,), (SX - 2) * SY), wb1[...])
    core[...] = (conv + blocks(own[SY : SX * SY - SY]).astype(F32)).astype(BF16)
    band(w2t, wb2)
    lab = labels[...].reshape(SX * SY, SZ).T
    ids = iota((slots, SX * SY), 0)
    count = jnp.zeros((slots, SX * SY), F32)
    for z in range(SZ):
        hit = jnp.broadcast_to(lab[z : z + 1, :], (slots, SX * SY)) == ids
        hot = hit.astype(F32)
        count = count + hot
        odd, half, b = z % 2, z // 2 % 2, z // 4
        at = b * 256 + half * 128
        member[odd * slots : (odd + 1) * slots, at : at + 128] = hot.astype(BF16)
    count = jnp.sum(count, axis=1, keepdims=True)
    li = lists[...]
    rows = home.shape[0]
    which = (iota((rows, slots), 0) == jnp.broadcast_to(li >> 7, (rows, slots))).astype(BF16)
    table = home[...]
    high = (table >> 6).astype(F32).T.astype(BF16)
    low = (table & 63).astype(F32).T.astype(BF16)
    lane = iota((128, slots), 0) == jnp.broadcast_to(li & 127, (128, slots))
    owner = jnp.sum(jnp.where(lane, dot(high, which), 0.0), axis=0, keepdims=True)
    row = jnp.sum(jnp.where(lane, dot(low, which), 0.0), axis=0, keepdims=True)
    across = jnp.broadcast_to(owner, (slots, slots))
    same = (across.T == across) & (iota((slots, slots), 0) < iota((slots, slots), 1))
    rank = jnp.sum(same.astype(F32), axis=0, keepdims=True)
    at = (owner * CAP + rank).astype(jnp.int32)
    total = place.shape[0]
    place[...] = (
        (iota((total, slots), 0) == jnp.broadcast_to(at, (total, slots))).astype(F32).astype(BF16)
    )
    key = jnp.broadcast_to(row + 1.0, (128, slots)).T
    count = jnp.broadcast_to(count, (slots, 128))
    big = jnp.floor(count * (1.0 / 64.0))
    lanes = iota((slots, 128), 1)
    info = jnp.where(lanes == 64, key, 0.0)
    info = jnp.where(lanes == 65, big, info)
    info = jnp.where(lanes == 66, count - 64.0 * big, info)
    meta[...] = info.astype(BF16)


def before(begun, v, labels, lists, home, w1t, w2t, devices):
    slots = lists.shape[1]
    return pl.pallas_call(
        before_kernel,
        out_shape=(
            jax.ShapeDtypeStruct((3456, 256), BF16),
            jax.ShapeDtypeStruct((3456, 256), BF16),
            jax.ShapeDtypeStruct((2 * slots, 2 * NB * SX * SY), BF16),
            jax.ShapeDtypeStruct((devices * CAP, slots), BF16),
            jax.ShapeDtypeStruct((slots, 128), BF16),
            jax.ShapeDtypeStruct((NB * (SX - 2) * SY, 256), BF16),
        ),
        in_specs=[VMEM] * 7,
        out_specs=(VMEM,) * 6,
        scratch_shapes=[pltpu.VMEM((SX * SY, WIDE), BF16)] * 3,
        compiler_params=params(),
        cost_estimate=pl.CostEstimate(flops=10**8, bytes_accessed=8 * 2**20, transcendentals=0),
        name="before",
    )(begun, v, labels, lists, home, w1t, w2t)


def choose(flag, yes, no):
    return jnp.where(flag, yes.astype(F32), no.astype(F32)).astype(BF16)


def x_extended(even, v, xa, xb):
    a = xa[...]
    b = xb[...]
    low = choose(even, b, a)
    high = choose(even, a, b)
    return jnp.concatenate([low, v[...], high], axis=0)


def columns_kernel(where, v, xa, xb, near, far):
    x_even = where[0] % 2 == 0
    y_even = where[1] % 2 == 0
    block = x_extended(x_even, v, xa, xb).reshape(EX * SY, LANES)
    r = iota((64, EX * SY), 0)
    c = r // 16
    y = jnp.where(c < 2, c, c + 12)
    pick = ((r % 16) * 16 + y == iota((64, EX * SY), 1)).astype(F32).astype(BF16)
    cols = dot(pick, block).astype(BF16)

    @pl.when(y_even)
    def _():
        near[...] = cols[32:64]
        far[...] = cols[0:32]

    @pl.when(jnp.logical_not(y_even))
    def _():
        near[...] = cols[0:32]
        far[...] = cols[32:64]


def columns(where, v, xa, xb):
    shape = jax.ShapeDtypeStruct((32, LANES), BF16)
    return pl.pallas_call(
        columns_kernel,
        out_shape=(shape, shape),
        in_specs=[SMEM, VMEM, VMEM, VMEM],
        out_specs=(VMEM, VMEM),
        compiler_params=params(),
        name="columns",
    )(where, v, xa, xb)


def slabs_kernel(where, v, xa, xb, core, near, far, wb, a0, a1, a2, own, cols, s0, s1, s2):
    gx, last_x = where[0], where[2] - 1
    x_even, y_even = where[0] % 2 == 0, where[1] % 2 == 0
    a, b = xa[...], xb[...]
    block = jnp.concatenate(
        [choose(x_even, b, a), v[0:2], v[SX - 2 : SX], choose(x_even, a, b)], axis=0
    ).reshape(8 * SY, LANES)
    s0[...], s1[...], s2[...] = shifts_y(widen(relu(block)))
    conv = dot(windows((s0, s1, s2), (0, 4 * SY), 2 * SY), wb[...])
    residual = jnp.concatenate([block[SY : 3 * SY], block[5 * SY : 7 * SY]], axis=0)
    x = iota((NB * 4 * SY, 256), 0) // SY % 4
    inside = ((x > 0) | (gx > 0)) & ((x < 3) | (gx < last_x))
    sides = jnp.where(inside, conv + blocks(residual).astype(F32), 0.0).astype(BF16)
    sides = unblocks(sides)
    main = jnp.concatenate([sides[0 : 2 * SY], unblocks(core[...]), sides[2 * SY :]], axis=0)
    own[...] = main[SY : SY + SX * SY]
    a0[...], a1[...], a2[...] = shifts_y(widen(relu(main)))
    low = choose(y_even, far[...], near[...])
    high = choose(y_even, near[...], far[...])
    side = relu(jnp.concatenate([low, high], axis=0))
    store_rolled(cols, widen(side))


def store_rolled(ref, wide):
    n = wide.shape[0]
    ref[0] = wide
    for kx in (1, 2):
        ref[kx] = pltpu.roll(wide, n - kx, 0)


def slabs(where, v, xa, xb, core, near, far, wb):
    full = jax.ShapeDtypeStruct((FX * SY, WIDE), BF16)
    return pl.pallas_call(
        slabs_kernel,
        out_shape=(
            full,
            full,
            full,
            jax.ShapeDtypeStruct((SX * SY, LANES), BF16),
            jax.ShapeDtypeStruct((3, 64, WIDE), BF16),
        ),
        in_specs=[SMEM] + [VMEM] * 7,
        out_specs=(VMEM,) * 5,
        scratch_shapes=[pltpu.VMEM((8 * SY, WIDE), BF16)] * 3,
        compiler_params=params(),
        cost_estimate=pl.CostEstimate(flops=2 * 10**9, bytes_accessed=2**20, transcendentals=0),
        name="slabs",
    )(where, v, xa, xb, core, near, far, wb)


def outer_kernel(
    where, a0i, a1i, a2i, owni, cols, near, far, ya, yb, wb1, a0, a1, a2, own, halo
):
    gx, gy = where[0], where[1]
    last_x, last_y = where[2] - 1, where[3] - 1
    y_even = gy % 2 == 0
    low = choose(y_even, yb[...], ya[...])
    high = choose(y_even, ya[...], yb[...])
    own_low = choose(y_even, far[...], near[...])
    own_high = choose(y_even, near[...], far[...])
    store_rolled(halo, widen(relu(jnp.concatenate([low, high], axis=0))))
    at = [(halo, 0), (halo, 16), (cols, 0), (cols, 16), (cols, 32), (cols, 48), (halo, 32), (halo, 48)]

    def group(g, kx, b):
        ref, start = at[g]
        return ref[kx, start : start + 16, 256 * b : 256 * b + 384]

    left = jnp.concatenate(
        [
            jnp.concatenate(
                [group(g + ky, kx, b) for ky in range(3) for kx in range(3)], axis=1
            )
            for b in range(NB)
            for g in (0, 1, 4, 5)
        ],
        axis=0,
    )
    conv = dot(left, wb1[...])
    residual = jnp.concatenate([low[16:32], own_low[0:16], own_high[16:32], high[0:16]], axis=0)
    residual = pltpu.roll(residual, 63, 0)
    row = iota((NB * 64, 256), 0)
    x = row % 16
    g = row // 16 % 4
    inside = ((x > 0) | (gx > 0)) & ((x < FX - 1) | (gx < last_x))
    inside = inside & ((g > 0) | (gy > 0)) & ((g < 3) | (gy < last_y))
    edge = jnp.where(inside, conv + blocks(residual).astype(F32), 0.0).astype(BF16)
    edge = unblocks(edge)
    wide = widen(relu(edge))
    for x in range(FX):
        s = SY * x
        a0[s : s + 1] = wide[x : x + 1]
        a0[s + 1 : s + 2] = wide[16 + x : 17 + x]
        a1[s : s + 1] = wide[16 + x : 17 + x]
        a1[s + SY - 1 : s + SY] = wide[32 + x : 33 + x]
        a2[s + SY - 2 : s + SY - 1] = wide[32 + x : 33 + x]
        a2[s + SY - 1 : s + SY] = wide[48 + x : 49 + x]
    for x in range(SX):
        s = SY * x
        own[s : s + 1] = edge[17 + x : 18 + x]
        own[s + SY - 1 : s + SY] = edge[33 + x : 34 + x]


def outer(where, a0, a1, a2, own, cols, near, far, ya, yb, wb1, wb2, member, place, meta):
    full = jax.ShapeDtypeStruct(a0.shape, BF16)
    a0, a1, a2, own = pl.pallas_call(
        outer_kernel,
        out_shape=(full, full, full, jax.ShapeDtypeStruct(own.shape, BF16)),
        in_specs=[SMEM] + [VMEM] * 10,
        out_specs=(VMEM,) * 4,
        scratch_shapes=[pltpu.VMEM((3, 64, WIDE), BF16)],
        input_output_aliases={1: 0, 2: 1, 3: 2, 4: 3},
        compiler_params=params(),
        name="outer",
    )(where, a0, a1, a2, own, cols, near, far, ya, yb, wb1)
    return pl.pallas_call(
        second_kernel,
        out_shape=jax.ShapeDtypeStruct((place.shape[0], 128), BF16),
        in_specs=[VMEM] * 8,
        out_specs=VMEM,
        scratch_shapes=[
            pltpu.VMEM((2 * meta.shape[0], 128), F32),
            pltpu.VMEM((256 * STEP, 128), BF16),
        ],
        compiler_params=params(),
        name="second",
    )(a0, a1, a2, own, wb2, member, place, meta)


def second_kernel(a0, a1, a2, own, wb2, member, place, meta, out, both, fresh):
    slots = meta.shape[0]
    both[...] = jnp.zeros_like(both)

    def block(i, carry):
        first = i * STEP
        left = jnp.concatenate(
            [
                jnp.concatenate(
                    [
                        ref[kx * SY : kx * SY + SX * SY, pl.ds(pl.multiple_of(256 * (first + b), 256), 384)]
                        for ref in (a0, a1, a2)
                        for kx in range(3)
                    ],
                    axis=1,
                )
                for b in range(STEP)
            ],
            axis=0,
        )
        conv = dot(left, wb2[...])
        for b in range(STEP):
            at = pl.multiple_of(256 * (first + b), 256)
            second = conv[128 * b : 128 * b + 128] + own[:, pl.ds(at, 256)].astype(F32)
            fresh[256 * b : 256 * b + 128] = second[:, 0:128].astype(BF16)
            fresh[256 * b + 128 : 256 * b + 256] = second[:, 128:256].astype(BF16)
        both[...] += dot(member[:, pl.ds(pl.multiple_of(256 * first, 256), 256 * STEP)], fresh[...])
        return carry

    lax.fori_loop(0, NB // STEP, block, 0)
    lanes = iota((slots, 128), 1)
    sums = both[0:slots] + pltpu.roll(both[slots : 2 * slots], 64, 1)
    rows = jnp.where(lanes < CH, sums, meta[...].astype(F32)).astype(BF16)
    out[...] = dot(place[...], rows).astype(BF16)


def head_kernel(got, w_in, w_out, out):
    rows = got[...]
    n = rows.shape[0]
    seg = out.shape[0]
    unit = (iota((8, 128), 1) == CH).astype(F32).astype(BF16)
    key = lax.dot_general(unit, rows, (((1,), (1,)), ((), ())), preferred_element_type=F32)
    key = jnp.broadcast_to(key[0:1], (seg, n))
    hit = (key == (iota((seg, n), 0) + 1).astype(F32)).astype(F32).astype(BF16)
    total = dot(hit, rows)
    lanes = iota((seg, 128), 1)
    digits = jnp.where(lanes == CH + 1, total * 64.0, jnp.where(lanes == CH + 2, total, 0.0))
    count = jnp.sum(digits, axis=1, keepdims=True)
    means = (total[:, 0:CH] / jnp.maximum(count, 1.0)).astype(BF16)
    hidden = jnp.maximum(dot(means, w_in[...]), 0.0).astype(BF16)
    out[...] = dot(hidden, w_out[...]).astype(BF16)


def head(got, w_in, w_out, seg):
    return pl.pallas_call(
        head_kernel,
        out_shape=jax.ShapeDtypeStruct((seg, w_out.shape[1]), BF16),
        in_specs=[VMEM] * 3,
        out_specs=VMEM,
        compiler_params=params(),
        name="head",
    )(got, w_in, w_out)


def pairs(count):
    inner_pairs = [(i, i ^ 1) for i in range(count)]
    outer_pairs = [(i, i + 1 if i % 2 else i - 1) for i in range(1, count - 1)]
    return inner_pairs, outer_pairs


def local(n_gx, n_gy, features, labels, lists, home, conv_first, conv_second, head_in, head_out):
    gx = lax.axis_index("gx")
    gy = lax.axis_index("gy")
    devices = n_gx * n_gy
    where = jnp.stack([gx, gy, jnp.int32(n_gx), jnp.int32(n_gy)]).astype(jnp.int32)
    even = gx % 2 == 0
    to_a = lax.dynamic_slice_in_dim(features, jnp.where(even, SX - 2, 0), 2, 0)
    to_b = lax.dynamic_slice_in_dim(features, jnp.where(even, 0, SX - 2), 2, 0)
    inner_x, outer_x = pairs(n_gx)
    inner_y, outer_y = pairs(n_gy)
    xa = lax.ppermute(to_a, "gx", inner_x)
    xb = lax.ppermute(to_b, "gx", outer_x)
    wb1, wb2, member, place, meta, core = before(
        begin(), features, labels, lists, home.reshape(-1, 128), conv_first.T, conv_second.T, devices
    )
    near, far = columns(where, features, xa, xb)
    ya = lax.ppermute(near, "gy", inner_y)
    yb = lax.ppermute(far, "gy", outer_y)
    a0, a1, a2, own, cols = slabs(where, features, xa, xb, core, near, far, wb1)
    rows = outer(where, a0, a1, a2, own, cols, near, far, ya, yb, wb1, wb2, member, place, meta)
    rows = rows.reshape(devices, CAP, 128)
    got = lax.all_to_all(rows, ("gx", "gy"), 0, 0, tiled=True)
    return head(got.reshape(devices * CAP, 128), head_in, head_out, home.size // devices)


def solution(mesh):
    placed = (
        P("gx", "gy", None),
        P("gx", "gy", None),
        P(("gx", "gy"), None),
        P(),
        P(),
        P(),
        P(),
        P(),
    )
    return jax.shard_map(
        functools.partial(local, mesh.shape["gx"], mesh.shape["gy"]),
        mesh=mesh,
        in_specs=placed,
        out_specs=P(("gx", "gy"), None),
        check_vma=False,
    )
```

```python
import functools

import jax
import jax.numpy as jnp
from jax import lax
from jax.experimental import pallas as pl
from jax.experimental.pallas import tpu as pltpu
from jax.sharding import PartitionSpec as P

F32 = jnp.float32
BF16 = jnp.bfloat16
SX, SY, SZ, CH = 8, 16, 32, 64
LANES = SZ * CH
WIDE = LANES + 2 * CH
NB = 8
EX = SX + 4
FX = SX + 2
CAP = 8
VMEM = pl.BlockSpec(memory_space=pltpu.VMEM)
SMEM = pl.BlockSpec(memory_space=pltpu.SMEM)


def params(mb=20):
    return pltpu.CompilerParams(vmem_limit_bytes=mb * 2**20)


def iota(shape, dim):
    return lax.broadcasted_iota(jnp.int32, shape, dim)


def dot(a, b):
    return jnp.dot(a, b, preferred_element_type=F32)


def widen(rows):
    zero = jnp.zeros((rows.shape[0], CH), rows.dtype)
    return jnp.concatenate([zero, rows, zero], axis=1)


def relu(rows):
    return jnp.maximum(rows, jnp.zeros_like(rows))


def begin_kernel(out):
    pass


def begin():
    return pl.pallas_call(
        begin_kernel,
        out_shape=jax.ShapeDtypeStruct((12 * 2**20,), F32),
        out_specs=pl.BlockSpec(memory_space=pl.ANY),
        cost_estimate=pl.CostEstimate(flops=10**10, bytes_accessed=4096, transcendentals=0),
        name="begin",
    )()


def band(wt_ref, out_ref):
    weight = wt_ref[...].astype(F32).T.astype(BF16)
    zero = jnp.zeros((CH, CH), BF16)
    quiet = jnp.zeros((128, 128), BF16)
    for kx in range(3):
        for ky in range(3):
            start = (kx * 3 + ky) * 3 * CH
            w = weight[start : start + 3 * CH, :]
            both = jnp.concatenate(
                [jnp.concatenate([w, zero], axis=0), jnp.concatenate([zero, w], axis=0)], axis=1
            )
            base = (ky * 3 + kx) * 384
            out_ref[base : base + 256, 0:128] = both
            out_ref[base + 128 : base + 384, 128:256] = both
            out_ref[base + 256 : base + 384, 0:128] = quiet
            out_ref[base : base + 128, 128:256] = quiet


def blocks(rows):
    return jnp.concatenate([rows[:, 256 * b : 256 * b + 256] for b in range(NB)], axis=0)


def unblocks(stack):
    n = stack.shape[0] // NB
    return jnp.concatenate([stack[n * b : n * b + n] for b in range(NB)], axis=1)


def shifts_y(wide):
    n = wide.shape[0]
    grid = wide.reshape(n // SY, SY, WIDE)
    zero = jnp.zeros((n // SY, 1, WIDE), wide.dtype)
    below = jnp.concatenate([zero, grid[:, : SY - 1]], axis=1).reshape(n, WIDE)
    above = jnp.concatenate([grid[:, 1:], zero], axis=1).reshape(n, WIDE)
    return below, wide, above


def windows(shifted, starts, rows):
    parts = []
    for b in range(NB):
        for start in starts:
            parts.append(
                jnp.concatenate(
                    [
                        ref[start + kx * SY : start + kx * SY + rows, 256 * b : 256 * b + 384]
                        for ref in shifted
                        for kx in range(3)
                    ],
                    axis=1,
                )
            )
    return jnp.concatenate(parts, axis=0)


def before_kernel(begun, v, labels, lists, home, w1t, w2t, wb1, wb2, member, place, meta, core, s0, s1, s2):
    slots = lists.shape[1]
    band(w1t, wb1)
    own = v[...].reshape(SX * SY, LANES)
    s0[...], s1[...], s2[...] = shifts_y(widen(relu(own)))
    conv = dot(windows((s0, s1, s2), (0,), (SX - 2) * SY), wb1[...])
    core[...] = (conv + blocks(own[SY : SX * SY - SY]).astype(F32)).astype(BF16)
    band(w2t, wb2)
    lab = labels[...].reshape(SX * SY, SZ).T
    ids = iota((slots, SX * SY), 0)
    count = jnp.zeros((slots, SX * SY), F32)
    for z in range(SZ):
        hit = jnp.broadcast_to(lab[z : z + 1, :], (slots, SX * SY)) == ids
        hot = hit.astype(F32)
        count = count + hot
        odd, half, b = z % 2, z // 2 % 2, z // 4
        at = b * 256 + half * 128
        member[odd * slots : (odd + 1) * slots, at : at + 128] = hot.astype(BF16)
    count = jnp.sum(count, axis=1, keepdims=True)
    li = lists[...]
    rows = home.shape[0]
    which = (iota((rows, slots), 0) == jnp.broadcast_to(li >> 7, (rows, slots))).astype(BF16)
    table = home[...]
    high = (table >> 6).astype(F32).T.astype(BF16)
    low = (table & 63).astype(F32).T.astype(BF16)
    lane = iota((128, slots), 0) == jnp.broadcast_to(li & 127, (128, slots))
    owner = jnp.sum(jnp.where(lane, dot(high, which), 0.0), axis=0, keepdims=True)
    row = jnp.sum(jnp.where(lane, dot(low, which), 0.0), axis=0, keepdims=True)
    across = jnp.broadcast_to(owner, (slots, slots))
    same = (across.T == across) & (iota((slots, slots), 0) < iota((slots, slots), 1))
    rank = jnp.sum(same.astype(F32), axis=0, keepdims=True)
    at = (owner * CAP + rank).astype(jnp.int32)
    total = place.shape[0]
    place[...] = (
        (iota((total, slots), 0) == jnp.broadcast_to(at, (total, slots))).astype(F32).astype(BF16)
    )
    key = jnp.broadcast_to(row + 1.0, (128, slots)).T
    count = jnp.broadcast_to(count, (slots, 128))
    big = jnp.floor(count * (1.0 / 64.0))
    lanes = iota((slots, 128), 1)
    info = jnp.where(lanes == 64, key, 0.0)
    info = jnp.where(lanes == 65, big, info)
    info = jnp.where(lanes == 66, count - 64.0 * big, info)
    meta[...] = info.astype(BF16)


def before(begun, v, labels, lists, home, w1t, w2t, devices):
    slots = lists.shape[1]
    return pl.pallas_call(
        before_kernel,
        out_shape=(
            jax.ShapeDtypeStruct((3456, 256), BF16),
            jax.ShapeDtypeStruct((3456, 256), BF16),
            jax.ShapeDtypeStruct((2 * slots, 2 * NB * SX * SY), BF16),
            jax.ShapeDtypeStruct((devices * CAP, slots), BF16),
            jax.ShapeDtypeStruct((slots, 128), BF16),
            jax.ShapeDtypeStruct((NB * (SX - 2) * SY, 256), BF16),
        ),
        in_specs=[pl.BlockSpec(memory_space=pl.ANY)] + [VMEM] * 6,
        out_specs=(VMEM,) * 6,
        scratch_shapes=[pltpu.VMEM((SX * SY, WIDE), BF16)] * 3,
        compiler_params=params(),
        cost_estimate=pl.CostEstimate(flops=10**8, bytes_accessed=8 * 2**20, transcendentals=0),
        name="before",
    )(begun, v, labels, lists, home, w1t, w2t)


def choose(flag, yes, no):
    return jnp.where(flag, yes.astype(F32), no.astype(F32)).astype(BF16)


def x_extended(even, v, xa, xb):
    a = xa[...]
    b = xb[...]
    low = choose(even, b, a)
    high = choose(even, a, b)
    return jnp.concatenate([low, v[...], high], axis=0)


def columns_kernel(where, v, xb, xa, near, far):
    x_even = where[0] % 2 == 0
    y_even = where[1] % 2 == 0
    block = x_extended(x_even, v, xa, xb).reshape(EX * SY, LANES)
    r = iota((64, EX * SY), 0)
    c = r // 16
    y = jnp.where(c < 2, c, c + 12)
    pick = ((r % 16) * 16 + y == iota((64, EX * SY), 1)).astype(F32).astype(BF16)
    cols = dot(pick, block).astype(BF16)

    @pl.when(y_even)
    def _():
        near[...] = cols[32:64]
        far[...] = cols[0:32]

    @pl.when(jnp.logical_not(y_even))
    def _():
        near[...] = cols[0:32]
        far[...] = cols[32:64]


def columns(where, v, xa, xb):
    shape = jax.ShapeDtypeStruct((32, LANES), BF16)
    return pl.pallas_call(
        columns_kernel,
        out_shape=(shape, shape),
        in_specs=[SMEM, VMEM, VMEM, VMEM],
        out_specs=(VMEM, VMEM),
        compiler_params=params(),
        name="columns",
    )(where, v, xb, xa)


def slabs_kernel(where, v, xb, xa, core, near, far, wb, a0, a1, a2, own, cols, s0, s1, s2):
    gx, last_x = where[0], where[2] - 1
    x_even, y_even = where[0] % 2 == 0, where[1] % 2 == 0
    a, b = xa[...], xb[...]
    block = jnp.concatenate(
        [choose(x_even, b, a), v[0:2], v[SX - 2 : SX], choose(x_even, a, b)], axis=0
    ).reshape(8 * SY, LANES)
    s0[...], s1[...], s2[...] = shifts_y(widen(relu(block)))
    conv = dot(windows((s0, s1, s2), (0, 4 * SY), 2 * SY), wb[...])
    residual = jnp.concatenate([block[SY : 3 * SY], block[5 * SY : 7 * SY]], axis=0)
    x = iota((NB * 4 * SY, 256), 0) // SY % 4
    inside = ((x > 0) | (gx > 0)) & ((x < 3) | (gx < last_x))
    sides = jnp.where(inside, conv + blocks(residual).astype(F32), 0.0).astype(BF16)
    sides = unblocks(sides)
    main = jnp.concatenate([sides[0 : 2 * SY], unblocks(core[...]), sides[2 * SY :]], axis=0)
    own[...] = main[SY : SY + SX * SY]
    a0[...], a1[...], a2[...] = shifts_y(widen(relu(main)))
    low = choose(y_even, far[...], near[...])
    high = choose(y_even, near[...], far[...])
    side = relu(jnp.concatenate([low, high], axis=0))
    store_rolled(cols, widen(side))


def store_rolled(ref, wide):
    n = wide.shape[0]
    ref[0] = wide
    for kx in (1, 2):
        ref[kx] = pltpu.roll(wide, n - kx, 0)


def slabs(where, v, xa, xb, core, near, far, wb):
    full = jax.ShapeDtypeStruct((FX * SY, WIDE), BF16)
    return pl.pallas_call(
        slabs_kernel,
        out_shape=(
            full,
            full,
            full,
            jax.ShapeDtypeStruct((SX * SY, LANES), BF16),
            jax.ShapeDtypeStruct((3, 64, WIDE), BF16),
        ),
        in_specs=[SMEM] + [VMEM] * 7,
        out_specs=(VMEM,) * 5,
        scratch_shapes=[pltpu.VMEM((8 * SY, WIDE), BF16)] * 3,
        compiler_params=params(),
        cost_estimate=pl.CostEstimate(flops=2 * 10**9, bytes_accessed=2**20, transcendentals=0),
        name="slabs",
    )(where, v, xb, xa, core, near, far, wb)


def outer_kernel(
    where, a0i, a1i, a2i, owni, cols, near, far, ya, yb, wb1, a0, a1, a2, own, halo
):
    gx, gy = where[0], where[1]
    last_x, last_y = where[2] - 1, where[3] - 1
    y_even = gy % 2 == 0
    low = choose(y_even, yb[...], ya[...])
    high = choose(y_even, ya[...], yb[...])
    own_low = choose(y_even, far[...], near[...])
    own_high = choose(y_even, near[...], far[...])
    store_rolled(halo, widen(relu(jnp.concatenate([low, high], axis=0))))
    at = [(halo, 0), (halo, 16), (cols, 0), (cols, 16), (cols, 32), (cols, 48), (halo, 32), (halo, 48)]

    def group(g, kx, b):
        ref, start = at[g]
        return ref[kx, start : start + 16, 256 * b : 256 * b + 384]

    left = jnp.concatenate(
        [
            jnp.concatenate(
                [group(g + ky, kx, b) for ky in range(3) for kx in range(3)], axis=1
            )
            for b in range(NB)
            for g in (0, 1, 4, 5)
        ],
        axis=0,
    )
    conv = dot(left, wb1[...])
    residual = jnp.concatenate([low[16:32], own_low[0:16], own_high[16:32], high[0:16]], axis=0)
    residual = pltpu.roll(residual, 63, 0)
    row = iota((NB * 64, 256), 0)
    x = row % 16
    g = row // 16 % 4
    inside = ((x > 0) | (gx > 0)) & ((x < FX - 1) | (gx < last_x))
    inside = inside & ((g > 0) | (gy > 0)) & ((g < 3) | (gy < last_y))
    edge = jnp.where(inside, conv + blocks(residual).astype(F32), 0.0).astype(BF16)
    edge = unblocks(edge)
    wide = widen(relu(edge))
    for x in range(FX):
        s = SY * x
        a0[s : s + 1] = wide[x : x + 1]
        a0[s + 1 : s + 2] = wide[16 + x : 17 + x]
        a1[s : s + 1] = wide[16 + x : 17 + x]
        a1[s + SY - 1 : s + SY] = wide[32 + x : 33 + x]
        a2[s + SY - 2 : s + SY - 1] = wide[32 + x : 33 + x]
        a2[s + SY - 1 : s + SY] = wide[48 + x : 49 + x]
    for x in range(SX):
        s = SY * x
        own[s : s + 1] = edge[17 + x : 18 + x]
        own[s + SY - 1 : s + SY] = edge[33 + x : 34 + x]


def outer(where, a0, a1, a2, own, cols, near, far, ya, yb, wb1, wb2, member, place, meta):
    full = jax.ShapeDtypeStruct(a0.shape, BF16)
    a0, a1, a2, own = pl.pallas_call(
        outer_kernel,
        out_shape=(full, full, full, jax.ShapeDtypeStruct(own.shape, BF16)),
        in_specs=[SMEM] + [VMEM] * 10,
        out_specs=(VMEM,) * 4,
        scratch_shapes=[pltpu.VMEM((3, 64, WIDE), BF16)],
        input_output_aliases={1: 0, 2: 1, 3: 2, 4: 3},
        compiler_params=params(),
        name="outer",
    )(where, a0, a1, a2, own, cols, near, far, ya, yb, wb1)
    return pl.pallas_call(
        second_kernel,
        out_shape=jax.ShapeDtypeStruct((place.shape[0], 128), BF16),
        in_specs=[VMEM] * 8,
        out_specs=VMEM,
        scratch_shapes=[pltpu.VMEM((256 * NB, 128), BF16)],
        compiler_params=params(),
        name="second",
    )(a0, a1, a2, own, wb2, member, place, meta)


def second_kernel(a0, a1, a2, own, wb2, member, place, meta, out, fresh):
    slots = meta.shape[0]
    for b in range(NB):
        at = 256 * b
        left = jnp.concatenate(
            [
                ref[kx * SY : kx * SY + SX * SY, at : at + 384]
                for ref in (a0, a1, a2)
                for kx in range(3)
            ],
            axis=1,
        )
        second = dot(left, wb2[...]) + own[:, at : at + 256].astype(F32)
        fresh[at : at + 128] = second[:, 0:128].astype(BF16)
        fresh[at + 128 : at + 256] = second[:, 128:256].astype(BF16)
    both = dot(member[...], fresh[...])
    lanes = iota((slots, 128), 1)
    sums = both[0:slots] + pltpu.roll(both[slots : 2 * slots], 64, 1)
    rows = jnp.where(lanes < CH, sums, meta[...].astype(F32)).astype(BF16)
    out[...] = dot(place[...], rows).astype(BF16)


def head_kernel(got, w_in, w_out, out):
    rows = got[...]
    n = rows.shape[0]
    seg = out.shape[0]
    unit = (iota((8, 128), 1) == CH).astype(F32).astype(BF16)
    key = lax.dot_general(unit, rows, (((1,), (1,)), ((), ())), preferred_element_type=F32)
    key = jnp.broadcast_to(key[0:1], (seg, n))
    hit = (key == (iota((seg, n), 0) + 1).astype(F32)).astype(F32).astype(BF16)
    total = dot(hit, rows)
    lanes = iota((seg, 128), 1)
    digits = jnp.where(lanes == CH + 1, total * 64.0, jnp.where(lanes == CH + 2, total, 0.0))
    count = jnp.sum(digits, axis=1, keepdims=True)
    means = (total[:, 0:CH] / jnp.maximum(count, 1.0)).astype(BF16)
    hidden = jnp.maximum(dot(means, w_in[...]), 0.0).astype(BF16)
    out[...] = dot(hidden, w_out[...]).astype(BF16)


def head(got, w_in, w_out, seg):
    return pl.pallas_call(
        head_kernel,
        out_shape=jax.ShapeDtypeStruct((seg, w_out.shape[1]), BF16),
        in_specs=[VMEM] * 3,
        out_specs=VMEM,
        compiler_params=params(),
        name="head",
    )(got, w_in, w_out)


def pairs(count):
    inner_pairs = [(i, i ^ 1) for i in range(count)]
    outer_pairs = [(i, i + 1 if i % 2 else i - 1) for i in range(1, count - 1)]
    return inner_pairs, outer_pairs


def local(n_gx, n_gy, features, labels, lists, home, conv_first, conv_second, head_in, head_out):
    gx = lax.axis_index("gx")
    gy = lax.axis_index("gy")
    devices = n_gx * n_gy
    where = jnp.stack([gx, gy, jnp.int32(n_gx), jnp.int32(n_gy)]).astype(jnp.int32)
    even = gx % 2 == 0
    to_a = lax.dynamic_slice_in_dim(features, jnp.where(even, SX - 2, 0), 2, 0)
    to_b = lax.dynamic_slice_in_dim(features, jnp.where(even, 0, SX - 2), 2, 0)
    inner_x, outer_x = pairs(n_gx)
    inner_y, outer_y = pairs(n_gy)
    xb = lax.ppermute(to_b, "gx", outer_x)
    xa = lax.ppermute(to_a, "gx", inner_x)
    wb1, wb2, member, place, meta, core = before(
        begin(), features, labels, lists, home.reshape(-1, 128), conv_first.T, conv_second.T, devices
    )
    near, far = columns(where, features, xa, xb)
    yb = lax.ppermute(far, "gy", outer_y)
    ya = lax.ppermute(near, "gy", inner_y)
    a0, a1, a2, own, cols = slabs(where, features, xa, xb, core, near, far, wb1)
    rows = outer(where, a0, a1, a2, own, cols, near, far, ya, yb, wb1, wb2, member, place, meta)
    rows = rows.reshape(devices, CAP, 128)
    got = lax.all_to_all(rows, ("gx", "gy"), 0, 0, tiled=True)
    return head(got.reshape(devices * CAP, 128), head_in, head_out, home.size // devices)


def solution(mesh):
    placed = (
        P("gx", "gy", None),
        P("gx", "gy", None),
        P(("gx", "gy"), None),
        P(),
        P(),
        P(),
        P(),
        P(),
    )
    return jax.shard_map(
        functools.partial(local, mesh.shape["gx"], mesh.shape["gy"]),
        mesh=mesh,
        in_specs=placed,
        out_specs=P(("gx", "gy"), None),
        check_vma=False,
    )
```

```python
import functools

import jax
import jax.numpy as jnp
from jax import lax
from jax.experimental import pallas as pl
from jax.experimental.pallas import tpu as pltpu
from jax.sharding import PartitionSpec as P

F32 = jnp.float32
BF16 = jnp.bfloat16
SX, SY, SZ, CH = 8, 16, 32, 64
LANES = SZ * CH
WIDE = LANES + 2 * CH
NB = 8
EX = SX + 4
FX = SX + 2
CAP = 8
VMEM = pl.BlockSpec(memory_space=pltpu.VMEM)
SMEM = pl.BlockSpec(memory_space=pltpu.SMEM)


def params(mb=20):
    return pltpu.CompilerParams(vmem_limit_bytes=mb * 2**20)


def iota(shape, dim):
    return lax.broadcasted_iota(jnp.int32, shape, dim)


def dot(a, b):
    return jnp.dot(a, b, preferred_element_type=F32)


def widen(rows):
    zero = jnp.zeros((rows.shape[0], CH), rows.dtype)
    return jnp.concatenate([zero, rows, zero], axis=1)


def relu(rows):
    return jnp.maximum(rows, jnp.zeros_like(rows))


def begin_kernel(out):
    pass


def begin():
    return pl.pallas_call(
        begin_kernel,
        out_shape=jax.ShapeDtypeStruct((12 * 2**20,), F32),
        out_specs=pl.BlockSpec(memory_space=pl.ANY),
        cost_estimate=pl.CostEstimate(flops=10**10, bytes_accessed=4096, transcendentals=0),
        name="begin",
    )()


def column_of(r):
    c, x = r // 16, r % 16
    return c, x, jnp.where(c < 2, c, c + SY - 4)


def band(wt_ref, out_ref):
    weight = wt_ref[...].astype(F32).T.astype(BF16)
    zero = jnp.zeros((CH, CH), BF16)
    quiet = jnp.zeros((128, 128), BF16)
    for kx in range(3):
        for ky in range(3):
            start = (kx * 3 + ky) * 3 * CH
            w = weight[start : start + 3 * CH, :]
            both = jnp.concatenate(
                [jnp.concatenate([w, zero], axis=0), jnp.concatenate([zero, w], axis=0)], axis=1
            )
            base = (ky * 3 + kx) * 384
            out_ref[base : base + 256, 0:128] = both
            out_ref[base + 128 : base + 384, 128:256] = both
            out_ref[base + 256 : base + 384, 0:128] = quiet
            out_ref[base : base + 128, 128:256] = quiet


def blocks(rows):
    return jnp.concatenate([rows[:, 256 * b : 256 * b + 256] for b in range(NB)], axis=0)


def unblocks(stack):
    n = stack.shape[0] // NB
    return jnp.concatenate([stack[n * b : n * b + n] for b in range(NB)], axis=1)


def shifts_y(wide):
    n = wide.shape[0]
    grid = wide.reshape(n // SY, SY, WIDE)
    zero = jnp.zeros((n // SY, 1, WIDE), wide.dtype)
    below = jnp.concatenate([zero, grid[:, : SY - 1]], axis=1).reshape(n, WIDE)
    above = jnp.concatenate([grid[:, 1:], zero], axis=1).reshape(n, WIDE)
    return below, wide, above


def convolve(shifted, starts, rows, weight, step):
    parts = []
    for first in range(0, NB, step):
        left = jnp.concatenate(
            [
                jnp.concatenate(
                    [
                        ref[start + kx * SY : start + kx * SY + rows, 256 * b : 256 * b + 384]
                        for ref in shifted
                        for kx in range(3)
                    ],
                    axis=1,
                )
                for b in range(first, first + step)
                for start in starts
            ],
            axis=0,
        )
        parts.append(dot(left, weight[...]))
    return jnp.concatenate(parts, axis=0)


def before_kernel(begun, v, labels, lists, home, w1t, w2t, wb1, wb2, member, place, meta, core, mine, s0, s1, s2):
    slots = lists.shape[1]
    band(w1t, wb1)
    own = v[...].reshape(SX * SY, LANES)
    s0[...], s1[...], s2[...] = shifts_y(widen(relu(own)))
    conv = convolve((s0, s1, s2), (0,), (SX - 2) * SY, wb1, 4)
    core[...] = (conv + blocks(own[SY : SX * SY - SY]).astype(F32)).astype(BF16)
    band(w2t, wb2)
    c, x, y = column_of(iota((64, SX * SY), 0))
    pick = ((x - 2) * SY + y == iota((64, SX * SY), 1)) & (x >= 2) & (x < EX - 2)
    mine[...] = dot(pick.astype(F32).astype(BF16), own)
    lab = labels[...].reshape(SX * SY, SZ).T
    ids = iota((slots, SX * SY), 0)
    count = jnp.zeros((slots, SX * SY), F32)
    for z in range(SZ):
        hit = jnp.broadcast_to(lab[z : z + 1, :], (slots, SX * SY)) == ids
        hot = hit.astype(F32)
        count = count + hot
        odd, half, b = z % 2, z // 2 % 2, z // 4
        at = b * 256 + half * 128
        member[odd * slots : (odd + 1) * slots, at : at + 128] = hot.astype(BF16)
    count = jnp.sum(count, axis=1, keepdims=True)
    li = lists[...]
    rows = home.shape[0]
    which = (iota((rows, slots), 0) == jnp.broadcast_to(li >> 7, (rows, slots))).astype(BF16)
    table = home[...]
    high = (table >> 6).astype(F32).T.astype(BF16)
    low = (table & 63).astype(F32).T.astype(BF16)
    lane = iota((128, slots), 0) == jnp.broadcast_to(li & 127, (128, slots))
    owner = jnp.sum(jnp.where(lane, dot(high, which), 0.0), axis=0, keepdims=True)
    row = jnp.sum(jnp.where(lane, dot(low, which), 0.0), axis=0, keepdims=True)
    across = jnp.broadcast_to(owner, (slots, slots))
    same = (across.T == across) & (iota((slots, slots), 0) < iota((slots, slots), 1))
    rank = jnp.sum(same.astype(F32), axis=0, keepdims=True)
    at = (owner * CAP + rank).astype(jnp.int32)
    total = place.shape[0]
    place[...] = (
        (iota((total, slots), 0) == jnp.broadcast_to(at, (total, slots))).astype(F32).astype(BF16)
    )
    key = jnp.broadcast_to(row + 1.0, (128, slots)).T
    count = jnp.broadcast_to(count, (slots, 128))
    big = jnp.floor(count * (1.0 / 64.0))
    lanes = iota((slots, 128), 1)
    info = jnp.where(lanes == 64, key, 0.0)
    info = jnp.where(lanes == 65, big, info)
    info = jnp.where(lanes == 66, count - 64.0 * big, info)
    meta[...] = info.astype(BF16)


def before(begun, v, labels, lists, home, w1t, w2t, devices):
    slots = lists.shape[1]
    return pl.pallas_call(
        before_kernel,
        out_shape=(
            jax.ShapeDtypeStruct((3456, 256), BF16),
            jax.ShapeDtypeStruct((3456, 256), BF16),
            jax.ShapeDtypeStruct((2 * slots, 2 * NB * SX * SY), BF16),
            jax.ShapeDtypeStruct((devices * CAP, slots), BF16),
            jax.ShapeDtypeStruct((slots, 128), BF16),
            jax.ShapeDtypeStruct((NB * (SX - 2) * SY, 256), BF16),
            jax.ShapeDtypeStruct((64, LANES), F32),
        ),
        in_specs=[pl.BlockSpec(memory_space=pl.ANY)] + [VMEM] * 6,
        out_specs=(VMEM,) * 7,
        scratch_shapes=[pltpu.VMEM((SX * SY, WIDE), BF16)] * 3,
        compiler_params=params(),
        cost_estimate=pl.CostEstimate(flops=10**8, bytes_accessed=8 * 2**20, transcendentals=0),
        name="before",
    )(begun, v, labels, lists, home, w1t, w2t)


def choose(flag, yes, no):
    return jnp.where(flag, yes.astype(F32), no.astype(F32)).astype(BF16)


def columns_kernel(where, mine, xb, xa, near, far):
    x_even = where[0] % 2 == 0
    y_even = where[1] % 2 == 0
    sides = jnp.concatenate([xa[...], xb[...]], axis=0).reshape(4 * SY, LANES)
    c, x, y = column_of(iota((64, 4 * SY), 0))
    k = jnp.where(x < 2, x, jnp.where((x >= EX - 2) & (x < EX), x - SX, -1))
    k = jnp.where(x_even, jnp.where(k >= 2, k - 2, jnp.where(k >= 0, k + 2, -1)), k)
    pick = ((k * SY + y == iota((64, 4 * SY), 1)) & (k >= 0)).astype(F32).astype(BF16)
    cols = (mine[...] + dot(pick, sides)).astype(BF16)

    @pl.when(y_even)
    def _():
        near[...] = cols[32:64]
        far[...] = cols[0:32]

    @pl.when(jnp.logical_not(y_even))
    def _():
        near[...] = cols[0:32]
        far[...] = cols[32:64]


def columns(where, mine, xb, xa):
    shape = jax.ShapeDtypeStruct((32, LANES), BF16)
    return pl.pallas_call(
        columns_kernel,
        out_shape=(shape, shape),
        in_specs=[SMEM, VMEM, VMEM, VMEM],
        out_specs=(VMEM, VMEM),
        compiler_params=params(),
        name="columns",
    )(where, mine, xb, xa)


def slabs_kernel(where, v, xa, xb, core, near, far, wb, a0, a1, a2, own, cols, raw, s0, s1, s2):
    gx, last_x = where[0], where[2] - 1
    x_even, y_even = where[0] % 2 == 0, where[1] % 2 == 0
    a, b = xa[...], xb[...]
    block = jnp.concatenate(
        [choose(x_even, b, a), v[0:2], v[SX - 2 : SX], choose(x_even, a, b)], axis=0
    ).reshape(8 * SY, LANES)
    s0[...], s1[...], s2[...] = shifts_y(widen(relu(block)))
    conv = convolve((s0, s1, s2), (0, 4 * SY), 2 * SY, wb, 2)
    residual = jnp.concatenate([block[SY : 3 * SY], block[5 * SY : 7 * SY]], axis=0)
    x = iota((NB * 4 * SY, 256), 0) // SY % 4
    inside = ((x > 0) | (gx > 0)) & ((x < 3) | (gx < last_x))
    sides = jnp.where(inside, conv + blocks(residual).astype(F32), 0.0).astype(BF16)
    sides = unblocks(sides)
    main = jnp.concatenate([sides[0 : 2 * SY], unblocks(core[...]), sides[2 * SY :]], axis=0)
    own[...] = main[SY : SY + SX * SY]
    a0[...], a1[...], a2[...] = shifts_y(widen(relu(main)))
    low = choose(y_even, far[...], near[...])
    high = choose(y_even, near[...], far[...])
    side = jnp.concatenate([low, high], axis=0)
    raw[...] = side
    side = relu(side)
    store_rolled(cols, widen(side))


def store_rolled(ref, wide):
    n = wide.shape[0]
    ref[0] = wide
    for kx in (1, 2):
        ref[kx] = pltpu.roll(wide, n - kx, 0)


def slabs(where, v, xa, xb, core, near, far, wb):
    full = jax.ShapeDtypeStruct((FX * SY, WIDE), BF16)
    return pl.pallas_call(
        slabs_kernel,
        out_shape=(
            full,
            full,
            full,
            jax.ShapeDtypeStruct((SX * SY, LANES), BF16),
            jax.ShapeDtypeStruct((3, 64, WIDE), BF16),
            jax.ShapeDtypeStruct((64, LANES), BF16),
        ),
        in_specs=[SMEM] + [VMEM] * 7,
        out_specs=(VMEM,) * 6,
        scratch_shapes=[pltpu.VMEM((8 * SY, WIDE), BF16)] * 3,
        compiler_params=params(),
        cost_estimate=pl.CostEstimate(flops=2 * 10**9, bytes_accessed=2**20, transcendentals=0),
        name="slabs",
    )(where, v, xa, xb, core, near, far, wb)


def outer_kernel(
    where, a0i, a1i, a2i, owni, cols, raw, ya, yb, wb1, a0, a1, a2, own, halo
):
    gx, gy = where[0], where[1]
    last_x, last_y = where[2] - 1, where[3] - 1
    y_even = gy % 2 == 0
    low = choose(y_even, yb[...], ya[...])
    high = choose(y_even, ya[...], yb[...])
    store_rolled(halo, widen(relu(jnp.concatenate([low, high], axis=0))))
    at = [(halo, 0), (halo, 16), (cols, 0), (cols, 16), (cols, 32), (cols, 48), (halo, 32), (halo, 48)]

    def group(g, kx, b):
        ref, start = at[g]
        return ref[kx, start : start + 16, 256 * b : 256 * b + 384]

    left = jnp.concatenate(
        [
            jnp.concatenate(
                [group(g + ky, kx, b) for ky in range(3) for kx in range(3)], axis=1
            )
            for b in range(NB)
            for g in (0, 1, 4, 5)
        ],
        axis=0,
    )
    conv = dot(left, wb1[...])
    residual = jnp.concatenate([low[16:32], raw[0:16], raw[48:64], high[0:16]], axis=0)
    residual = pltpu.roll(residual, 63, 0)
    row = iota((NB * 64, 256), 0)
    x = row % 16
    g = row // 16 % 4
    inside = ((x > 0) | (gx > 0)) & ((x < FX - 1) | (gx < last_x))
    inside = inside & ((g > 0) | (gy > 0)) & ((g < 3) | (gy < last_y))
    edge = jnp.where(inside, conv + blocks(residual).astype(F32), 0.0).astype(BF16)
    edge = unblocks(edge)
    wide = widen(relu(edge))
    for x in range(FX):
        s = SY * x
        a0[s : s + 1] = wide[x : x + 1]
        a0[s + 1 : s + 2] = wide[16 + x : 17 + x]
        a1[s : s + 1] = wide[16 + x : 17 + x]
        a1[s + SY - 1 : s + SY] = wide[32 + x : 33 + x]
        a2[s + SY - 2 : s + SY - 1] = wide[32 + x : 33 + x]
        a2[s + SY - 1 : s + SY] = wide[48 + x : 49 + x]
    for x in range(SX):
        s = SY * x
        own[s : s + 1] = edge[17 + x : 18 + x]
        own[s + SY - 1 : s + SY] = edge[33 + x : 34 + x]


def outer(where, a0, a1, a2, own, cols, raw, ya, yb, wb1, wb2, member, place, meta):
    full = jax.ShapeDtypeStruct(a0.shape, BF16)
    a0, a1, a2, own = pl.pallas_call(
        outer_kernel,
        out_shape=(full, full, full, jax.ShapeDtypeStruct(own.shape, BF16)),
        in_specs=[SMEM] + [VMEM] * 9,
        out_specs=(VMEM,) * 4,
        scratch_shapes=[pltpu.VMEM((3, 64, WIDE), BF16)],
        input_output_aliases={1: 0, 2: 1, 3: 2, 4: 3},
        compiler_params=params(),
        name="outer",
    )(where, a0, a1, a2, own, cols, raw, ya, yb, wb1)
    return pl.pallas_call(
        second_kernel,
        out_shape=jax.ShapeDtypeStruct((place.shape[0], 128), BF16),
        in_specs=[VMEM] * 8,
        out_specs=VMEM,
        scratch_shapes=[pltpu.VMEM((256 * NB, 128), BF16)],
        compiler_params=params(),
        name="second",
    )(a0, a1, a2, own, wb2, member, place, meta)


def second_kernel(a0, a1, a2, own, wb2, member, place, meta, out, fresh):
    slots = meta.shape[0]
    for b in range(NB):
        at = 256 * b
        left = jnp.concatenate(
            [
                ref[kx * SY : kx * SY + SX * SY, at : at + 384]
                for ref in (a0, a1, a2)
                for kx in range(3)
            ],
            axis=1,
        )
        second = dot(left, wb2[...]) + own[:, at : at + 256].astype(F32)
        fresh[at : at + 128] = second[:, 0:128].astype(BF16)
        fresh[at + 128 : at + 256] = second[:, 128:256].astype(BF16)
    both = dot(member[...], fresh[...])
    lanes = iota((slots, 128), 1)
    sums = both[0:slots] + pltpu.roll(both[slots : 2 * slots], 64, 1)
    rows = jnp.where(lanes < CH, sums, meta[...].astype(F32)).astype(BF16)
    out[...] = dot(place[...], rows).astype(BF16)


def head_kernel(got, w_in, w_out, out):
    rows = got[...]
    n = rows.shape[0]
    seg = out.shape[0]
    unit = (iota((8, 128), 1) == CH).astype(F32).astype(BF16)
    key = lax.dot_general(unit, rows, (((1,), (1,)), ((), ())), preferred_element_type=F32)
    key = jnp.broadcast_to(key[0:1], (seg, n))
    hit = (key == (iota((seg, n), 0) + 1).astype(F32)).astype(F32).astype(BF16)
    total = dot(hit, rows)
    lanes = iota((seg, 128), 1)
    digits = jnp.where(lanes == CH + 1, total * 64.0, jnp.where(lanes == CH + 2, total, 0.0))
    count = jnp.sum(digits, axis=1, keepdims=True)
    means = (total[:, 0:CH] / jnp.maximum(count, 1.0)).astype(BF16)
    hidden = jnp.maximum(dot(means, w_in[...]), 0.0).astype(BF16)
    out[...] = dot(hidden, w_out[...]).astype(BF16)


def head(got, w_in, w_out, seg):
    return pl.pallas_call(
        head_kernel,
        out_shape=jax.ShapeDtypeStruct((seg, w_out.shape[1]), BF16),
        in_specs=[VMEM] * 3,
        out_specs=VMEM,
        compiler_params=params(),
        name="head",
    )(got, w_in, w_out)


def pairs(count):
    inner_pairs = [(i, i ^ 1) for i in range(count)]
    outer_pairs = [(i, i + 1 if i % 2 else i - 1) for i in range(1, count - 1)]
    return inner_pairs, outer_pairs


def local(n_gx, n_gy, features, labels, lists, home, conv_first, conv_second, head_in, head_out):
    gx = lax.axis_index("gx")
    gy = lax.axis_index("gy")
    devices = n_gx * n_gy
    where = jnp.stack([gx, gy, jnp.int32(n_gx), jnp.int32(n_gy)]).astype(jnp.int32)
    even = gx % 2 == 0
    to_a = lax.dynamic_slice_in_dim(features, jnp.where(even, SX - 2, 0), 2, 0)
    to_b = lax.dynamic_slice_in_dim(features, jnp.where(even, 0, SX - 2), 2, 0)
    inner_x, outer_x = pairs(n_gx)
    inner_y, outer_y = pairs(n_gy)
    xb = lax.ppermute(to_b, "gx", outer_x)
    xa = lax.ppermute(to_a, "gx", inner_x)
    wb1, wb2, member, place, meta, core, mine = before(
        begin(), features, labels, lists, home.reshape(-1, 128), conv_first.T, conv_second.T, devices
    )
    near, far = columns(where, mine, xb, xa)
    yb = lax.ppermute(far, "gy", outer_y)
    ya = lax.ppermute(near, "gy", inner_y)
    a0, a1, a2, own, cols, raw = slabs(where, features, xa, xb, core, near, far, wb1)
    rows = outer(where, a0, a1, a2, own, cols, raw, ya, yb, wb1, wb2, member, place, meta)
    rows = rows.reshape(devices, CAP, 128)
    got = lax.all_to_all(rows, ("gx", "gy"), 0, 0, tiled=True)
    return head(got.reshape(devices * CAP, 128), head_in, head_out, home.size // devices)


def solution(mesh):
    placed = (
        P("gx", "gy", None),
        P("gx", "gy", None),
        P(("gx", "gy"), None),
        P(),
        P(),
        P(),
        P(),
        P(),
    )
    return jax.shard_map(
        functools.partial(local, mesh.shape["gx"], mesh.shape["gy"]),
        mesh=mesh,
        in_specs=placed,
        out_specs=P(("gx", "gy"), None),
        check_vma=False,
    )
```

```python
import functools

import jax
import jax.numpy as jnp
from jax import lax
from jax.experimental import pallas as pl
from jax.experimental.pallas import tpu as pltpu
from jax.sharding import PartitionSpec as P

F32 = jnp.float32
BF16 = jnp.bfloat16
SX, SY, SZ, CH = 8, 16, 32, 64
LANES = SZ * CH
WIDE = LANES + 2 * CH
NB = 8
EX = SX + 4
FX = SX + 2
CAP = 8
VMEM = pl.BlockSpec(memory_space=pltpu.VMEM)
SMEM = pl.BlockSpec(memory_space=pltpu.SMEM)


def params(mb=20):
    return pltpu.CompilerParams(vmem_limit_bytes=mb * 2**20)


def iota(shape, dim):
    return lax.broadcasted_iota(jnp.int32, shape, dim)


def dot(a, b):
    return jnp.dot(a, b, preferred_element_type=F32)


def widen(rows):
    zero = jnp.zeros((rows.shape[0], CH), rows.dtype)
    return jnp.concatenate([zero, rows, zero], axis=1)


def relu(rows):
    return jnp.maximum(rows, jnp.zeros_like(rows))


def begin_kernel(out):
    pass


def begin():
    return pl.pallas_call(
        begin_kernel,
        out_shape=jax.ShapeDtypeStruct((12 * 2**20,), F32),
        out_specs=pl.BlockSpec(memory_space=pl.ANY),
        cost_estimate=pl.CostEstimate(flops=10**10, bytes_accessed=4096, transcendentals=0),
        name="begin",
    )()


def column_of(r):
    c, x = r // EX, r % EX
    return c, x, jnp.where(c < 2, c, c + SY - 4)


def band(wt_ref, out_ref):
    weight = wt_ref[...].astype(F32).T.astype(BF16)
    zero = jnp.zeros((CH, CH), BF16)
    quiet = jnp.zeros((128, 128), BF16)
    for kx in range(3):
        for ky in range(3):
            start = (kx * 3 + ky) * 3 * CH
            w = weight[start : start + 3 * CH, :]
            both = jnp.concatenate(
                [jnp.concatenate([w, zero], axis=0), jnp.concatenate([zero, w], axis=0)], axis=1
            )
            base = (ky * 3 + kx) * 384
            out_ref[base : base + 256, 0:128] = both
            out_ref[base + 128 : base + 384, 128:256] = both
            out_ref[base + 256 : base + 384, 0:128] = quiet
            out_ref[base : base + 128, 128:256] = quiet


def blocks(rows):
    return jnp.concatenate([rows[:, 256 * b : 256 * b + 256] for b in range(NB)], axis=0)


def unblocks(stack):
    n = stack.shape[0] // NB
    return jnp.concatenate([stack[n * b : n * b + n] for b in range(NB)], axis=1)


def shifts_y(wide):
    n = wide.shape[0]
    grid = wide.reshape(n // SY, SY, WIDE)
    zero = jnp.zeros((n // SY, 1, WIDE), wide.dtype)
    below = jnp.concatenate([zero, grid[:, : SY - 1]], axis=1).reshape(n, WIDE)
    above = jnp.concatenate([grid[:, 1:], zero], axis=1).reshape(n, WIDE)
    return below, wide, above


def convolve(shifted, starts, rows, weight, step):
    parts = []
    for first in range(0, NB, step):
        left = jnp.concatenate(
            [
                jnp.concatenate(
                    [
                        ref[start + kx * SY : start + kx * SY + rows, 256 * b : 256 * b + 384]
                        for ref in shifted
                        for kx in range(3)
                    ],
                    axis=1,
                )
                for b in range(first, first + step)
                for start in starts
            ],
            axis=0,
        )
        parts.append(dot(left, weight[...]))
    return jnp.concatenate(parts, axis=0)


def before_kernel(begun, v, labels, lists, home, w1t, w2t, wb1, wb2, member, place, meta, core, mine, s0, s1, s2):
    slots = lists.shape[1]
    band(w1t, wb1)
    own = v[...].reshape(SX * SY, LANES)
    s0[...], s1[...], s2[...] = shifts_y(widen(relu(own)))
    conv = convolve((s0, s1, s2), (0,), (SX - 2) * SY, wb1, 4)
    core[...] = (conv + blocks(own[SY : SX * SY - SY]).astype(F32)).astype(BF16)
    band(w2t, wb2)
    c, x, y = column_of(iota((4 * EX, SX * SY), 0))
    pick = ((x - 2) * SY + y == iota((4 * EX, SX * SY), 1)) & (x >= 2) & (x < EX - 2)
    mine[...] = dot(pick.astype(F32).astype(BF16), own)
    lab = labels[...].reshape(SX * SY, SZ).T
    ids = iota((slots, SX * SY), 0)
    count = jnp.zeros((slots, SX * SY), F32)
    for z in range(SZ):
        hit = jnp.broadcast_to(lab[z : z + 1, :], (slots, SX * SY)) == ids
        hot = hit.astype(F32)
        count = count + hot
        odd, half, b = z % 2, z // 2 % 2, z // 4
        at = b * 256 + half * 128
        member[odd * slots : (odd + 1) * slots, at : at + 128] = hot.astype(BF16)
    count = jnp.sum(count, axis=1, keepdims=True)
    li = lists[...]
    rows = home.shape[0]
    which = (iota((rows, slots), 0) == jnp.broadcast_to(li >> 7, (rows, slots))).astype(BF16)
    table = home[...]
    high = (table >> 6).astype(F32).T.astype(BF16)
    low = (table & 63).astype(F32).T.astype(BF16)
    lane = iota((128, slots), 0) == jnp.broadcast_to(li & 127, (128, slots))
    owner = jnp.sum(jnp.where(lane, dot(high, which), 0.0), axis=0, keepdims=True)
    row = jnp.sum(jnp.where(lane, dot(low, which), 0.0), axis=0, keepdims=True)
    across = jnp.broadcast_to(owner, (slots, slots))
    same = (across.T == across) & (iota((slots, slots), 0) < iota((slots, slots), 1))
    rank = jnp.sum(same.astype(F32), axis=0, keepdims=True)
    at = (owner * CAP + rank).astype(jnp.int32)
    total = place.shape[0]
    place[...] = (
        (iota((total, slots), 0) == jnp.broadcast_to(at, (total, slots))).astype(F32).astype(BF16)
    )
    key = jnp.broadcast_to(row + 1.0, (128, slots)).T
    count = jnp.broadcast_to(count, (slots, 128))
    big = jnp.floor(count * (1.0 / 64.0))
    lanes = iota((slots, 128), 1)
    info = jnp.where(lanes == 64, key, 0.0)
    info = jnp.where(lanes == 65, big, info)
    info = jnp.where(lanes == 66, count - 64.0 * big, info)
    meta[...] = info.astype(BF16)


def before(begun, v, labels, lists, home, w1t, w2t, devices):
    slots = lists.shape[1]
    return pl.pallas_call(
        before_kernel,
        out_shape=(
            jax.ShapeDtypeStruct((3456, 256), BF16),
            jax.ShapeDtypeStruct((3456, 256), BF16),
            jax.ShapeDtypeStruct((2 * slots, 2 * NB * SX * SY), BF16),
            jax.ShapeDtypeStruct((devices * CAP, slots), BF16),
            jax.ShapeDtypeStruct((slots, 128), BF16),
            jax.ShapeDtypeStruct((NB * (SX - 2) * SY, 256), BF16),
            jax.ShapeDtypeStruct((4 * EX, LANES), F32),
        ),
        in_specs=[pl.BlockSpec(memory_space=pl.ANY)] + [VMEM] * 6,
        out_specs=(VMEM,) * 7,
        scratch_shapes=[pltpu.VMEM((SX * SY, WIDE), BF16)] * 3,
        compiler_params=params(),
        cost_estimate=pl.CostEstimate(flops=10**8, bytes_accessed=8 * 2**20, transcendentals=0),
        name="before",
    )(begun, v, labels, lists, home, w1t, w2t)


def choose(flag, yes, no):
    return jnp.where(flag, yes.astype(F32), no.astype(F32)).astype(BF16)


def choose_columns(flag, yes, no):
    both = jnp.where(flag, yes.astype(F32), no.astype(F32))
    zero = jnp.zeros((16 - EX, LANES), F32)
    return jnp.concatenate([both[:EX], zero, both[EX:], zero], axis=0).astype(BF16)


def columns_kernel(where, mine, xb, xa, near, far):
    x_even = where[0] % 2 == 0
    y_even = where[1] % 2 == 0
    sides = jnp.concatenate([xa[...], xb[...]], axis=0).reshape(4 * SY, LANES)
    c, x, y = column_of(iota((4 * EX, 4 * SY), 0))
    k = jnp.where(x < 2, x, jnp.where((x >= EX - 2) & (x < EX), x - SX, -1))
    k = jnp.where(x_even, jnp.where(k >= 2, k - 2, jnp.where(k >= 0, k + 2, -1)), k)
    pick = ((k * SY + y == iota((4 * EX, 4 * SY), 1)) & (k >= 0)).astype(F32).astype(BF16)
    cols = (mine[...] + dot(pick, sides)).astype(BF16)

    @pl.when(y_even)
    def _():
        near[...] = cols[2 * EX :]
        far[...] = cols[: 2 * EX]

    @pl.when(jnp.logical_not(y_even))
    def _():
        near[...] = cols[: 2 * EX]
        far[...] = cols[2 * EX :]


def columns(where, mine, xb, xa):
    shape = jax.ShapeDtypeStruct((2 * EX, LANES), BF16)
    return pl.pallas_call(
        columns_kernel,
        out_shape=(shape, shape),
        in_specs=[SMEM, VMEM, VMEM, VMEM],
        out_specs=(VMEM, VMEM),
        compiler_params=params(),
        name="columns",
    )(where, mine, xb, xa)


def slabs_kernel(where, v, xa, xb, core, near, far, wb, a0, a1, a2, own, cols, raw, s0, s1, s2):
    gx, last_x = where[0], where[2] - 1
    x_even, y_even = where[0] % 2 == 0, where[1] % 2 == 0
    a, b = xa[...], xb[...]
    block = jnp.concatenate(
        [choose(x_even, b, a), v[0:2], v[SX - 2 : SX], choose(x_even, a, b)], axis=0
    ).reshape(8 * SY, LANES)
    s0[...], s1[...], s2[...] = shifts_y(widen(relu(block)))
    conv = convolve((s0, s1, s2), (0, 4 * SY), 2 * SY, wb, 2)
    residual = jnp.concatenate([block[SY : 3 * SY], block[5 * SY : 7 * SY]], axis=0)
    x = iota((NB * 4 * SY, 256), 0) // SY % 4
    inside = ((x > 0) | (gx > 0)) & ((x < 3) | (gx < last_x))
    sides = jnp.where(inside, conv + blocks(residual).astype(F32), 0.0).astype(BF16)
    sides = unblocks(sides)
    main = jnp.concatenate([sides[0 : 2 * SY], unblocks(core[...]), sides[2 * SY :]], axis=0)
    own[...] = main[SY : SY + SX * SY]
    a0[...], a1[...], a2[...] = shifts_y(widen(relu(main)))
    low = choose_columns(y_even, far[...], near[...])
    high = choose_columns(y_even, near[...], far[...])
    side = jnp.concatenate([low, high], axis=0)
    raw[...] = side
    side = relu(side)
    store_rolled(cols, widen(side))


def store_rolled(ref, wide):
    n = wide.shape[0]
    ref[0] = wide
    for kx in (1, 2):
        ref[kx] = pltpu.roll(wide, n - kx, 0)


def slabs(where, v, xa, xb, core, near, far, wb):
    full = jax.ShapeDtypeStruct((FX * SY, WIDE), BF16)
    return pl.pallas_call(
        slabs_kernel,
        out_shape=(
            full,
            full,
            full,
            jax.ShapeDtypeStruct((SX * SY, LANES), BF16),
            jax.ShapeDtypeStruct((3, 64, WIDE), BF16),
            jax.ShapeDtypeStruct((64, LANES), BF16),
        ),
        in_specs=[SMEM] + [VMEM] * 7,
        out_specs=(VMEM,) * 6,
        scratch_shapes=[pltpu.VMEM((8 * SY, WIDE), BF16)] * 3,
        compiler_params=params(),
        cost_estimate=pl.CostEstimate(flops=2 * 10**9, bytes_accessed=2**20, transcendentals=0),
        name="slabs",
    )(where, v, xa, xb, core, near, far, wb)


def outer_kernel(
    where, a0i, a1i, a2i, owni, cols, raw, ya, yb, wb1, a0, a1, a2, own, halo
):
    gx, gy = where[0], where[1]
    last_x, last_y = where[2] - 1, where[3] - 1
    y_even = gy % 2 == 0
    low = choose_columns(y_even, yb[...], ya[...])
    high = choose_columns(y_even, ya[...], yb[...])
    store_rolled(halo, widen(relu(jnp.concatenate([low, high], axis=0))))
    at = [(halo, 0), (halo, 16), (cols, 0), (cols, 16), (cols, 32), (cols, 48), (halo, 32), (halo, 48)]

    def group(g, kx, b):
        ref, start = at[g]
        return ref[kx, start : start + 16, 256 * b : 256 * b + 384]

    left = jnp.concatenate(
        [
            jnp.concatenate(
                [group(g + ky, kx, b) for ky in range(3) for kx in range(3)], axis=1
            )
            for b in range(NB)
            for g in (0, 1, 4, 5)
        ],
        axis=0,
    )
    conv = dot(left, wb1[...])
    residual = jnp.concatenate([low[16:32], raw[0:16], raw[48:64], high[0:16]], axis=0)
    residual = pltpu.roll(residual, 63, 0)
    row = iota((NB * 64, 256), 0)
    x = row % 16
    g = row // 16 % 4
    inside = ((x > 0) | (gx > 0)) & ((x < FX - 1) | (gx < last_x))
    inside = inside & ((g > 0) | (gy > 0)) & ((g < 3) | (gy < last_y))
    edge = jnp.where(inside, conv + blocks(residual).astype(F32), 0.0).astype(BF16)
    edge = unblocks(edge)
    wide = widen(relu(edge))
    for x in range(FX):
        s = SY * x
        a0[s : s + 1] = wide[x : x + 1]
        a0[s + 1 : s + 2] = wide[16 + x : 17 + x]
        a1[s : s + 1] = wide[16 + x : 17 + x]
        a1[s + SY - 1 : s + SY] = wide[32 + x : 33 + x]
        a2[s + SY - 2 : s + SY - 1] = wide[32 + x : 33 + x]
        a2[s + SY - 1 : s + SY] = wide[48 + x : 49 + x]
    for x in range(SX):
        s = SY * x
        own[s : s + 1] = edge[17 + x : 18 + x]
        own[s + SY - 1 : s + SY] = edge[33 + x : 34 + x]


def outer(where, a0, a1, a2, own, cols, raw, ya, yb, wb1, wb2, member, place, meta):
    full = jax.ShapeDtypeStruct(a0.shape, BF16)
    a0, a1, a2, own = pl.pallas_call(
        outer_kernel,
        out_shape=(full, full, full, jax.ShapeDtypeStruct(own.shape, BF16)),
        in_specs=[SMEM] + [VMEM] * 9,
        out_specs=(VMEM,) * 4,
        scratch_shapes=[pltpu.VMEM((3, 64, WIDE), BF16)],
        input_output_aliases={1: 0, 2: 1, 3: 2, 4: 3},
        compiler_params=params(),
        name="outer",
    )(where, a0, a1, a2, own, cols, raw, ya, yb, wb1)
    return pl.pallas_call(
        second_kernel,
        out_shape=jax.ShapeDtypeStruct((place.shape[0], 128), BF16),
        in_specs=[VMEM] * 8,
        out_specs=VMEM,
        scratch_shapes=[pltpu.VMEM((256 * NB, 128), BF16)],
        compiler_params=params(),
        name="second",
    )(a0, a1, a2, own, wb2, member, place, meta)


def second_kernel(a0, a1, a2, own, wb2, member, place, meta, out, fresh):
    slots = meta.shape[0]
    for b in range(NB):
        at = 256 * b
        left = jnp.concatenate(
            [
                ref[kx * SY : kx * SY + SX * SY, at : at + 384]
                for ref in (a0, a1, a2)
                for kx in range(3)
            ],
            axis=1,
        )
        second = dot(left, wb2[...]) + own[:, at : at + 256].astype(F32)
        fresh[at : at + 128] = second[:, 0:128].astype(BF16)
        fresh[at + 128 : at + 256] = second[:, 128:256].astype(BF16)
    both = dot(member[...], fresh[...])
    lanes = iota((slots, 128), 1)
    sums = both[0:slots] + pltpu.roll(both[slots : 2 * slots], 64, 1)
    rows = jnp.where(lanes < CH, sums, meta[...].astype(F32)).astype(BF16)
    out[...] = dot(place[...], rows).astype(BF16)


def head_kernel(got, w_in, w_out, out):
    rows = got[...]
    n = rows.shape[0]
    seg = out.shape[0]
    unit = (iota((8, 128), 1) == CH).astype(F32).astype(BF16)
    key = lax.dot_general(unit, rows, (((1,), (1,)), ((), ())), preferred_element_type=F32)
    key = jnp.broadcast_to(key[0:1], (seg, n))
    hit = (key == (iota((seg, n), 0) + 1).astype(F32)).astype(F32).astype(BF16)
    total = dot(hit, rows)
    lanes = iota((seg, 128), 1)
    digits = jnp.where(lanes == CH + 1, total * 64.0, jnp.where(lanes == CH + 2, total, 0.0))
    count = jnp.sum(digits, axis=1, keepdims=True)
    means = (total[:, 0:CH] / jnp.maximum(count, 1.0)).astype(BF16)
    hidden = jnp.maximum(dot(means, w_in[...]), 0.0).astype(BF16)
    out[...] = dot(hidden, w_out[...]).astype(BF16)


def head(got, w_in, w_out, seg):
    return pl.pallas_call(
        head_kernel,
        out_shape=jax.ShapeDtypeStruct((seg, w_out.shape[1]), BF16),
        in_specs=[VMEM] * 3,
        out_specs=VMEM,
        compiler_params=params(),
        name="head",
    )(got, w_in, w_out)


def pairs(count):
    inner_pairs = [(i, i ^ 1) for i in range(count)]
    outer_pairs = [(i, i + 1 if i % 2 else i - 1) for i in range(1, count - 1)]
    return inner_pairs, outer_pairs


def local(n_gx, n_gy, features, labels, lists, home, conv_first, conv_second, head_in, head_out):
    gx = lax.axis_index("gx")
    gy = lax.axis_index("gy")
    devices = n_gx * n_gy
    where = jnp.stack([gx, gy, jnp.int32(n_gx), jnp.int32(n_gy)]).astype(jnp.int32)
    even = gx % 2 == 0
    to_a = lax.dynamic_slice_in_dim(features, jnp.where(even, SX - 2, 0), 2, 0)
    to_b = lax.dynamic_slice_in_dim(features, jnp.where(even, 0, SX - 2), 2, 0)
    inner_x, outer_x = pairs(n_gx)
    inner_y, outer_y = pairs(n_gy)
    xb = lax.ppermute(to_b, "gx", outer_x)
    xa = lax.ppermute(to_a, "gx", inner_x)
    wb1, wb2, member, place, meta, core, mine = before(
        begin(), features, labels, lists, home.reshape(-1, 128), conv_first.T, conv_second.T, devices
    )
    near, far = columns(where, mine, xb, xa)
    yb = lax.ppermute(far, "gy", outer_y)
    ya = lax.ppermute(near, "gy", inner_y)
    a0, a1, a2, own, cols, raw = slabs(where, features, xa, xb, core, near, far, wb1)
    rows = outer(where, a0, a1, a2, own, cols, raw, ya, yb, wb1, wb2, member, place, meta)
    rows = rows.reshape(devices, CAP, 128)
    got = lax.all_to_all(rows, ("gx", "gy"), 0, 0, tiled=True)
    return head(got.reshape(devices * CAP, 128), head_in, head_out, home.size // devices)


def solution(mesh):
    placed = (
        P("gx", "gy", None),
        P("gx", "gy", None),
        P(("gx", "gy"), None),
        P(),
        P(),
        P(),
        P(),
        P(),
    )
    return jax.shard_map(
        functools.partial(local, mesh.shape["gx"], mesh.shape["gy"]),
        mesh=mesh,
        in_specs=placed,
        out_specs=P(("gx", "gy"), None),
        check_vma=False,
    )
```

```python
import functools

import jax
import jax.numpy as jnp
from jax import lax
from jax.experimental import pallas as pl
from jax.experimental.pallas import tpu as pltpu
from jax.sharding import PartitionSpec as P

F32 = jnp.float32
BF16 = jnp.bfloat16
SX, SY, SZ, CH = 8, 16, 32, 64
LANES = SZ * CH
WIDE = LANES + 2 * CH
NB = 8
EX = SX + 4
FX = SX + 2
CAP = 8
VMEM = pl.BlockSpec(memory_space=pltpu.VMEM)
SMEM = pl.BlockSpec(memory_space=pltpu.SMEM)


def params(mb=20):
    return pltpu.CompilerParams(vmem_limit_bytes=mb * 2**20)


def iota(shape, dim):
    return lax.broadcasted_iota(jnp.int32, shape, dim)


def dot(a, b):
    return jnp.dot(a, b, preferred_element_type=F32)


def widen(rows):
    zero = jnp.zeros((rows.shape[0], CH), rows.dtype)
    return jnp.concatenate([zero, rows, zero], axis=1)


def relu(rows):
    return jnp.maximum(rows, jnp.zeros_like(rows))


def begin_kernel(out):
    pass


def begin():
    return pl.pallas_call(
        begin_kernel,
        out_shape=jax.ShapeDtypeStruct((12 * 2**20,), F32),
        out_specs=pl.BlockSpec(memory_space=pl.ANY),
        cost_estimate=pl.CostEstimate(flops=10**10, bytes_accessed=4096, transcendentals=0),
        name="begin",
    )()


def column_of(r):
    c, x = r // EX, r % EX
    return c, x, jnp.where(c < 2, c, c + SY - 4)


def band(wt_ref, out_ref):
    weight = wt_ref[...].astype(F32).T.astype(BF16)
    zero = jnp.zeros((CH, CH), BF16)
    quiet = jnp.zeros((128, 128), BF16)
    for kx in range(3):
        for ky in range(3):
            start = (kx * 3 + ky) * 3 * CH
            w = weight[start : start + 3 * CH, :]
            both = jnp.concatenate(
                [jnp.concatenate([w, zero], axis=0), jnp.concatenate([zero, w], axis=0)], axis=1
            )
            base = (ky * 3 + kx) * 384
            out_ref[base : base + 256, 0:128] = both
            out_ref[base + 128 : base + 384, 128:256] = both
            out_ref[base + 256 : base + 384, 0:128] = quiet
            out_ref[base : base + 128, 128:256] = quiet


def blocks(rows):
    return jnp.concatenate([rows[:, 256 * b : 256 * b + 256] for b in range(NB)], axis=0)


def unblocks(stack):
    n = stack.shape[0] // NB
    return jnp.concatenate([stack[n * b : n * b + n] for b in range(NB)], axis=1)


def shifts_y(wide):
    n = wide.shape[0]
    grid = wide.reshape(n // SY, SY, WIDE)
    zero = jnp.zeros((n // SY, 1, WIDE), wide.dtype)
    below = jnp.concatenate([zero, grid[:, : SY - 1]], axis=1).reshape(n, WIDE)
    above = jnp.concatenate([grid[:, 1:], zero], axis=1).reshape(n, WIDE)
    return below, wide, above


def convolve(shifted, starts, rows, weight, step):
    parts = []
    for first in range(0, NB, step):
        left = jnp.concatenate(
            [
                jnp.concatenate(
                    [
                        ref[start + kx * SY : start + kx * SY + rows, 256 * b : 256 * b + 384]
                        for ref in shifted
                        for kx in range(3)
                    ],
                    axis=1,
                )
                for b in range(first, first + step)
                for start in starts
            ],
            axis=0,
        )
        parts.append(dot(left, weight[...]))
    return jnp.concatenate(parts, axis=0)


def before_kernel(begun, v, labels, lists, home, w1t, w2t, wb1, wb2, member, place, meta, core, mine, s0, s1, s2):
    slots = lists.shape[1]
    band(w1t, wb1)
    own = v[...].reshape(SX * SY, LANES)
    s0[...], s1[...], s2[...] = shifts_y(widen(relu(own)))
    conv = convolve((s0, s1, s2), (0,), (SX - 2) * SY, wb1, 4)
    core[...] = (conv + blocks(own[SY : SX * SY - SY]).astype(F32)).astype(BF16)
    band(w2t, wb2)
    c, x, y = column_of(iota((4 * EX, SX * SY), 0))
    pick = ((x - 2) * SY + y == iota((4 * EX, SX * SY), 1)) & (x >= 2) & (x < EX - 2)
    mine[...] = dot(pick.astype(F32).astype(BF16), own)
    lab = labels[...].reshape(SX * SY, SZ).T
    ids = iota((slots, SX * SY), 0)
    count = jnp.zeros((slots, SX * SY), F32)
    for z in range(SZ):
        hit = jnp.broadcast_to(lab[z : z + 1, :], (slots, SX * SY)) == ids
        hot = hit.astype(F32)
        count = count + hot
        odd, half, b = z % 2, z // 2 % 2, z // 4
        at = b * 256 + half * 128
        member[odd * slots : (odd + 1) * slots, at : at + 128] = hot.astype(BF16)
    count = jnp.sum(count, axis=1, keepdims=True)
    li = lists[...]
    rows = home.shape[0]
    which = (iota((rows, slots), 0) == jnp.broadcast_to(li >> 7, (rows, slots))).astype(BF16)
    table = home[...]
    high = (table >> 6).astype(F32).T.astype(BF16)
    low = (table & 63).astype(F32).T.astype(BF16)
    lane = iota((128, slots), 0) == jnp.broadcast_to(li & 127, (128, slots))
    owner = jnp.sum(jnp.where(lane, dot(high, which), 0.0), axis=0, keepdims=True)
    row = jnp.sum(jnp.where(lane, dot(low, which), 0.0), axis=0, keepdims=True)
    across = jnp.broadcast_to(owner, (slots, slots))
    same = (across.T == across) & (iota((slots, slots), 0) < iota((slots, slots), 1))
    rank = jnp.sum(same.astype(F32), axis=0, keepdims=True)
    at = (owner * CAP + rank).astype(jnp.int32)
    total = place.shape[0]
    place[...] = (
        (iota((total, slots), 0) == jnp.broadcast_to(at, (total, slots))).astype(F32).astype(BF16)
    )
    key = jnp.broadcast_to(row + 1.0, (128, slots)).T
    count = jnp.broadcast_to(count, (slots, 128))
    big = jnp.floor(count * (1.0 / 64.0))
    lanes = iota((slots, 128), 1)
    info = jnp.where(lanes == 64, key, 0.0)
    info = jnp.where(lanes == 65, big, info)
    info = jnp.where(lanes == 66, count - 64.0 * big, info)
    meta[...] = info.astype(BF16)


def before(begun, v, labels, lists, home, w1t, w2t, devices):
    slots = lists.shape[1]
    return pl.pallas_call(
        before_kernel,
        out_shape=(
            jax.ShapeDtypeStruct((3456, 256), BF16),
            jax.ShapeDtypeStruct((3456, 256), BF16),
            jax.ShapeDtypeStruct((2 * slots, 2 * NB * SX * SY), BF16),
            jax.ShapeDtypeStruct((devices * CAP, slots), BF16),
            jax.ShapeDtypeStruct((slots, 128), BF16),
            jax.ShapeDtypeStruct((NB * (SX - 2) * SY, 256), BF16),
            jax.ShapeDtypeStruct((4 * EX, LANES), F32),
        ),
        in_specs=[pl.BlockSpec(memory_space=pl.ANY)] + [VMEM] * 6,
        out_specs=(VMEM,) * 7,
        scratch_shapes=[pltpu.VMEM((SX * SY, WIDE), BF16)] * 3,
        compiler_params=params(),
        cost_estimate=pl.CostEstimate(flops=10**8, bytes_accessed=8 * 2**20, transcendentals=0),
        name="before",
    )(begun, v, labels, lists, home, w1t, w2t)


def choose(flag, yes, no):
    return jnp.where(flag, yes.astype(F32), no.astype(F32)).astype(BF16)


def choose_columns(flag, yes, no):
    both = jnp.where(flag, yes.astype(F32), no.astype(F32))
    zero = jnp.zeros((16 - EX, LANES), F32)
    return jnp.concatenate([both[:EX], zero, both[EX:], zero], axis=0).astype(BF16)


def columns_kernel(where, mine, xb, xa, near, far):
    x_even = where[0] % 2 == 0
    y_even = where[1] % 2 == 0
    sides = jnp.concatenate([xa[...], xb[...]], axis=0).reshape(4 * SY, LANES)
    c, x, y = column_of(iota((4 * EX, 4 * SY), 0))
    k = jnp.where(x < 2, x, jnp.where((x >= EX - 2) & (x < EX), x - SX, -1))
    k = jnp.where(x_even, jnp.where(k >= 2, k - 2, jnp.where(k >= 0, k + 2, -1)), k)
    pick = ((k * SY + y == iota((4 * EX, 4 * SY), 1)) & (k >= 0)).astype(F32).astype(BF16)
    cols = (mine[...] + dot(pick, sides)).astype(BF16)

    @pl.when(y_even)
    def _():
        near[...] = cols[2 * EX :]
        far[...] = cols[: 2 * EX]

    @pl.when(jnp.logical_not(y_even))
    def _():
        near[...] = cols[: 2 * EX]
        far[...] = cols[2 * EX :]


def columns(where, mine, xb, xa):
    shape = jax.ShapeDtypeStruct((2 * EX, LANES), BF16)
    return pl.pallas_call(
        columns_kernel,
        out_shape=(shape, shape),
        in_specs=[SMEM, VMEM, VMEM, VMEM],
        out_specs=(VMEM, VMEM),
        compiler_params=params(),
        name="columns",
    )(where, mine, xb, xa)


def slabs_kernel(where, v, xa, xb, core, near, far, wb, a0, a1, a2, own, cols, raw, s0, s1, s2):
    gx, last_x = where[0], where[2] - 1
    x_even, y_even = where[0] % 2 == 0, where[1] % 2 == 0
    a, b = xa[...], xb[...]
    block = jnp.concatenate(
        [choose(x_even, b, a), v[0:2], v[SX - 2 : SX], choose(x_even, a, b)], axis=0
    ).reshape(8 * SY, LANES)
    s0[...], s1[...], s2[...] = shifts_y(widen(relu(block)))
    conv = convolve((s0, s1, s2), (0, 4 * SY), 2 * SY, wb, 2)
    residual = jnp.concatenate([block[SY : 3 * SY], block[5 * SY : 7 * SY]], axis=0)
    x = iota((NB * 4 * SY, 256), 0) // SY % 4
    inside = ((x > 0) | (gx > 0)) & ((x < 3) | (gx < last_x))
    sides = jnp.where(inside, conv + blocks(residual).astype(F32), 0.0).astype(BF16)
    sides = unblocks(sides)
    main = jnp.concatenate([sides[0 : 2 * SY], unblocks(core[...]), sides[2 * SY :]], axis=0)
    own[...] = main[SY : SY + SX * SY]
    a0[...], a1[...], a2[...] = shifts_y(widen(relu(main)))
    low = choose_columns(y_even, far[...], near[...])
    high = choose_columns(y_even, near[...], far[...])
    side = jnp.concatenate([low, high], axis=0)
    raw[...] = side
    side = relu(side)
    store_rolled(cols, widen(side))


def store_rolled(ref, wide):
    n = wide.shape[0]
    ref[0] = wide
    for kx in (1, 2):
        ref[kx] = pltpu.roll(wide, n - kx, 0)


def slabs(where, v, xa, xb, core, near, far, wb):
    full = jax.ShapeDtypeStruct((FX * SY, WIDE), BF16)
    return pl.pallas_call(
        slabs_kernel,
        out_shape=(
            full,
            full,
            full,
            jax.ShapeDtypeStruct((SX * SY, LANES), BF16),
            jax.ShapeDtypeStruct((3, 64, WIDE), BF16),
            jax.ShapeDtypeStruct((64, LANES), BF16),
        ),
        in_specs=[SMEM] + [VMEM] * 7,
        out_specs=(VMEM,) * 6,
        scratch_shapes=[pltpu.VMEM((8 * SY, WIDE), BF16)] * 3,
        compiler_params=params(),
        cost_estimate=pl.CostEstimate(flops=2 * 10**9, bytes_accessed=2**20, transcendentals=0),
        name="slabs",
    )(where, v, xa, xb, core, near, far, wb)


def outer_kernel(
    where, a0i, a1i, a2i, owni, cols, raw, ya, yb, wb1, a0, a1, a2, own, halo
):
    gx, gy = where[0], where[1]
    last_x, last_y = where[2] - 1, where[3] - 1
    y_even = gy % 2 == 0
    low = choose_columns(y_even, yb[...], ya[...])
    high = choose_columns(y_even, ya[...], yb[...])
    store_rolled(halo, widen(relu(jnp.concatenate([low, high], axis=0))))
    at = [(halo, 0), (halo, 16), (cols, 0), (cols, 16), (cols, 32), (cols, 48), (halo, 32), (halo, 48)]

    def group(g, kx, b):
        ref, start = at[g]
        return ref[kx, start : start + 16, 256 * b : 256 * b + 384]

    left = jnp.concatenate(
        [
            jnp.concatenate(
                [group(g + ky, kx, b) for ky in range(3) for kx in range(3)], axis=1
            )
            for b in range(NB)
            for g in (0, 1, 4, 5)
        ],
        axis=0,
    )
    conv = dot(left, wb1[...])
    residual = jnp.concatenate([low[16:32], raw[0:16], raw[48:64], high[0:16]], axis=0)
    residual = pltpu.roll(residual, 63, 0)
    row = iota((NB * 64, 256), 0)
    x = row % 16
    g = row // 16 % 4
    inside = ((x > 0) | (gx > 0)) & ((x < FX - 1) | (gx < last_x))
    inside = inside & ((g > 0) | (gy > 0)) & ((g < 3) | (gy < last_y))
    edge = jnp.where(inside, conv + blocks(residual).astype(F32), 0.0).astype(BF16)
    edge = unblocks(edge)
    wide = widen(relu(edge))
    for x in range(FX):
        s = SY * x
        a0[s : s + 1] = wide[x : x + 1]
        a0[s + 1 : s + 2] = wide[16 + x : 17 + x]
        a1[s : s + 1] = wide[16 + x : 17 + x]
        a1[s + SY - 1 : s + SY] = wide[32 + x : 33 + x]
        a2[s + SY - 2 : s + SY - 1] = wide[32 + x : 33 + x]
        a2[s + SY - 1 : s + SY] = wide[48 + x : 49 + x]
    for x in range(SX):
        s = SY * x
        own[s : s + 1] = edge[17 + x : 18 + x]
        own[s + SY - 1 : s + SY] = edge[33 + x : 34 + x]


def outer(where, a0, a1, a2, own, cols, raw, ya, yb, wb1, wb2, member, place, meta):
    full = jax.ShapeDtypeStruct(a0.shape, BF16)
    a0, a1, a2, own = pl.pallas_call(
        outer_kernel,
        out_shape=(full, full, full, jax.ShapeDtypeStruct(own.shape, BF16)),
        in_specs=[SMEM] + [VMEM] * 9,
        out_specs=(VMEM,) * 4,
        scratch_shapes=[pltpu.VMEM((3, 64, WIDE), BF16)],
        input_output_aliases={1: 0, 2: 1, 3: 2, 4: 3},
        compiler_params=params(),
        name="outer",
    )(where, a0, a1, a2, own, cols, raw, ya, yb, wb1)
    return pl.pallas_call(
        second_kernel,
        out_shape=jax.ShapeDtypeStruct((place.shape[0], 128), BF16),
        in_specs=[VMEM] * 8,
        out_specs=VMEM,
        scratch_shapes=[pltpu.VMEM((256 * NB, 128), BF16)],
        compiler_params=params(),
        name="second",
    )(a0, a1, a2, own, wb2, member, place, meta)


def second_kernel(a0, a1, a2, own, wb2, member, place, meta, out, fresh):
    slots = meta.shape[0]
    for b in range(NB):
        at = 256 * b
        left = jnp.concatenate(
            [
                ref[kx * SY : kx * SY + SX * SY, at : at + 384]
                for ref in (a0, a1, a2)
                for kx in range(3)
            ],
            axis=1,
        )
        second = dot(left, wb2[...]) + own[:, at : at + 256].astype(F32)
        fresh[at : at + 128] = second[:, 0:128].astype(BF16)
        fresh[at + 128 : at + 256] = second[:, 128:256].astype(BF16)
    both = dot(member[...], fresh[...])
    lanes = iota((slots, 128), 1)
    sums = both[0:slots] + pltpu.roll(both[slots : 2 * slots], 64, 1)
    rows = jnp.where(lanes < CH, sums, meta[...].astype(F32)).astype(BF16)
    step = place.shape[0] // 4
    for k in range(4):
        at = k * step
        out[at : at + step] = dot(place[at : at + step], rows).astype(BF16)


def head_kernel(got, w_in, w_out, out):
    rows = got[...]
    n = rows.shape[0]
    seg = out.shape[0]
    unit = (iota((8, 128), 1) == CH).astype(F32).astype(BF16)
    key = lax.dot_general(unit, rows, (((1,), (1,)), ((), ())), preferred_element_type=F32)
    key = jnp.broadcast_to(key[0:1], (seg, n))
    hit = (key == (iota((seg, n), 0) + 1).astype(F32)).astype(F32).astype(BF16)
    total = dot(hit, rows)
    lanes = iota((seg, 128), 1)
    digits = jnp.where(lanes == CH + 1, total * 64.0, jnp.where(lanes == CH + 2, total, 0.0))
    count = jnp.sum(digits, axis=1, keepdims=True)
    means = (total[:, 0:CH] / jnp.maximum(count, 1.0)).astype(BF16)
    hidden = jnp.maximum(dot(means, w_in[...]), 0.0).astype(BF16)
    out[...] = dot(hidden, w_out[...]).astype(BF16)


def head(got, w_in, w_out, seg):
    return pl.pallas_call(
        head_kernel,
        out_shape=jax.ShapeDtypeStruct((seg, w_out.shape[1]), BF16),
        in_specs=[VMEM] * 3,
        out_specs=VMEM,
        compiler_params=params(),
        name="head",
    )(got, w_in, w_out)


def pairs(count):
    inner_pairs = [(i, i ^ 1) for i in range(count)]
    outer_pairs = [(i, i + 1 if i % 2 else i - 1) for i in range(1, count - 1)]
    return inner_pairs, outer_pairs


def local(n_gx, n_gy, features, labels, lists, home, conv_first, conv_second, head_in, head_out):
    gx = lax.axis_index("gx")
    gy = lax.axis_index("gy")
    devices = n_gx * n_gy
    where = jnp.stack([gx, gy, jnp.int32(n_gx), jnp.int32(n_gy)]).astype(jnp.int32)
    even = gx % 2 == 0
    to_a = lax.dynamic_slice_in_dim(features, jnp.where(even, SX - 2, 0), 2, 0)
    to_b = lax.dynamic_slice_in_dim(features, jnp.where(even, 0, SX - 2), 2, 0)
    inner_x, outer_x = pairs(n_gx)
    inner_y, outer_y = pairs(n_gy)
    xb = lax.ppermute(to_b, "gx", outer_x)
    xa = lax.ppermute(to_a, "gx", inner_x)
    wb1, wb2, member, place, meta, core, mine = before(
        begin(), features, labels, lists, home.reshape(-1, 128), conv_first.T, conv_second.T, devices
    )
    near, far = columns(where, mine, xb, xa)
    yb = lax.ppermute(far, "gy", outer_y)
    ya = lax.ppermute(near, "gy", inner_y)
    a0, a1, a2, own, cols, raw = slabs(where, features, xa, xb, core, near, far, wb1)
    rows = outer(where, a0, a1, a2, own, cols, raw, ya, yb, wb1, wb2, member, place, meta)
    rows = rows.reshape(devices, CAP, 128)
    got = lax.all_to_all(rows, ("gx", "gy"), 0, 0, tiled=True)
    return head(got.reshape(devices * CAP, 128), head_in, head_out, home.size // devices)


def solution(mesh):
    placed = (
        P("gx", "gy", None),
        P("gx", "gy", None),
        P(("gx", "gy"), None),
        P(),
        P(),
        P(),
        P(),
        P(),
    )
    return jax.shard_map(
        functools.partial(local, mesh.shape["gx"], mesh.shape["gy"]),
        mesh=mesh,
        in_specs=placed,
        out_specs=P(("gx", "gy"), None),
        check_vma=False,
    )
```

```python
import functools

import jax
import jax.numpy as jnp
from jax import lax
from jax.experimental import pallas as pl
from jax.experimental.pallas import tpu as pltpu
from jax.sharding import PartitionSpec as P

F32 = jnp.float32
BF16 = jnp.bfloat16
SX, SY, SZ, CH = 8, 16, 32, 64
LANES = SZ * CH
WIDE = LANES + 2 * CH
NB = 8
EX = SX + 4
FX = SX + 2
CAP = 8
VMEM = pl.BlockSpec(memory_space=pltpu.VMEM)
SMEM = pl.BlockSpec(memory_space=pltpu.SMEM)


def params(mb=20):
    return pltpu.CompilerParams(vmem_limit_bytes=mb * 2**20)


def iota(shape, dim):
    return lax.broadcasted_iota(jnp.int32, shape, dim)


def dot(a, b):
    return jnp.dot(a, b, preferred_element_type=F32)


def widen(rows):
    zero = jnp.zeros((rows.shape[0], CH), rows.dtype)
    return jnp.concatenate([zero, rows, zero], axis=1)


def relu(rows):
    return jnp.maximum(rows, jnp.zeros_like(rows))


def begin_kernel(out):
    pass


def begin():
    return pl.pallas_call(
        begin_kernel,
        out_shape=jax.ShapeDtypeStruct((12 * 2**20,), F32),
        out_specs=pl.BlockSpec(memory_space=pl.ANY),
        cost_estimate=pl.CostEstimate(flops=10**10, bytes_accessed=4096, transcendentals=0),
        name="begin",
    )()


def column_of(r):
    c, x = r // EX, r % EX
    return c, x, jnp.where(c < 2, c, c + SY - 4)


def band(wt_ref, out_ref):
    weight = wt_ref[...].astype(F32).T.astype(BF16)
    zero = jnp.zeros((CH, CH), BF16)
    quiet = jnp.zeros((128, 128), BF16)
    for kx in range(3):
        for ky in range(3):
            start = (kx * 3 + ky) * 3 * CH
            w = weight[start : start + 3 * CH, :]
            both = jnp.concatenate(
                [jnp.concatenate([w, zero], axis=0), jnp.concatenate([zero, w], axis=0)], axis=1
            )
            base = (ky * 3 + kx) * 384
            out_ref[base : base + 256, 0:128] = both
            out_ref[base + 128 : base + 384, 128:256] = both
            out_ref[base + 256 : base + 384, 0:128] = quiet
            out_ref[base : base + 128, 128:256] = quiet


def blocks(rows):
    return jnp.concatenate([rows[:, 256 * b : 256 * b + 256] for b in range(NB)], axis=0)


def unblocks(stack):
    n = stack.shape[0] // NB
    return jnp.concatenate([stack[n * b : n * b + n] for b in range(NB)], axis=1)


def shifts_y(wide):
    n = wide.shape[0]
    grid = wide.reshape(n // SY, SY, WIDE)
    zero = jnp.zeros((n // SY, 1, WIDE), wide.dtype)
    below = jnp.concatenate([zero, grid[:, : SY - 1]], axis=1).reshape(n, WIDE)
    above = jnp.concatenate([grid[:, 1:], zero], axis=1).reshape(n, WIDE)
    return below, wide, above


def convolve(shifted, starts, rows, weight, step):
    parts = []
    for first in range(0, NB, step):
        left = jnp.concatenate(
            [
                jnp.concatenate(
                    [
                        ref[start + kx * SY : start + kx * SY + rows, 256 * b : 256 * b + 384]
                        for ref in shifted
                        for kx in range(3)
                    ],
                    axis=1,
                )
                for b in range(first, first + step)
                for start in starts
            ],
            axis=0,
        )
        parts.append(dot(left, weight[...]))
    return jnp.concatenate(parts, axis=0)


def before_kernel(begun, v, labels, lists, home, w1t, w2t, wb1, wb2, member, place, meta, core, mine, s0, s1, s2):
    slots = lists.shape[1]
    band(w1t, wb1)
    own = v[...].reshape(SX * SY, LANES)
    s0[...], s1[...], s2[...] = shifts_y(widen(relu(own)))
    conv = convolve((s0, s1, s2), (0,), (SX - 2) * SY, wb1, 4)
    core[...] = (conv + blocks(own[SY : SX * SY - SY]).astype(F32)).astype(BF16)
    band(w2t, wb2)
    c, x, y = column_of(iota((4 * EX, SX * SY), 0))
    pick = ((x - 2) * SY + y == iota((4 * EX, SX * SY), 1)) & (x >= 2) & (x < EX - 2)
    mine[...] = dot(pick.astype(F32).astype(BF16), own)
    lab = labels[...].reshape(SX * SY, SZ).T
    ids = iota((slots, SX * SY), 0)
    count = jnp.zeros((slots, SX * SY), F32)
    for z in range(SZ):
        hit = jnp.broadcast_to(lab[z : z + 1, :], (slots, SX * SY)) == ids
        hot = hit.astype(F32)
        count = count + hot
        odd, half, b = z % 2, z // 2 % 2, z // 4
        at = b * 256 + half * 128
        member[odd * slots : (odd + 1) * slots, at : at + 128] = hot.astype(BF16)
    count = jnp.sum(count, axis=1, keepdims=True)
    li = lists[...]
    rows = home.shape[0]
    which = (iota((rows, slots), 0) == jnp.broadcast_to(li >> 7, (rows, slots))).astype(BF16)
    table = home[...]
    high = (table >> 6).astype(F32).T.astype(BF16)
    low = (table & 63).astype(F32).T.astype(BF16)
    lane = iota((128, slots), 0) == jnp.broadcast_to(li & 127, (128, slots))
    owner = jnp.sum(jnp.where(lane, dot(high, which), 0.0), axis=0, keepdims=True)
    row = jnp.sum(jnp.where(lane, dot(low, which), 0.0), axis=0, keepdims=True)
    across = jnp.broadcast_to(owner, (slots, slots))
    same = (across.T == across) & (iota((slots, slots), 0) < iota((slots, slots), 1))
    rank = jnp.sum(same.astype(F32), axis=0, keepdims=True)
    at = (owner * CAP + rank).astype(jnp.int32)
    total = place.shape[0]
    place[...] = (
        (iota((total, slots), 0) == jnp.broadcast_to(at, (total, slots))).astype(F32).astype(BF16)
    )
    key = jnp.broadcast_to(row + 1.0, (128, slots)).T
    count = jnp.broadcast_to(count, (slots, 128))
    big = jnp.floor(count * (1.0 / 64.0))
    lanes = iota((slots, 128), 1)
    info = jnp.where(lanes == 64, key, 0.0)
    info = jnp.where(lanes == 65, big, info)
    info = jnp.where(lanes == 66, count - 64.0 * big, info)
    meta[...] = info.astype(BF16)


def before(begun, v, labels, lists, home, w1t, w2t, devices):
    slots = lists.shape[1]
    return pl.pallas_call(
        before_kernel,
        out_shape=(
            jax.ShapeDtypeStruct((3456, 256), BF16),
            jax.ShapeDtypeStruct((3456, 256), BF16),
            jax.ShapeDtypeStruct((2 * slots, 2 * NB * SX * SY), BF16),
            jax.ShapeDtypeStruct((devices * CAP, slots), BF16),
            jax.ShapeDtypeStruct((slots, 128), BF16),
            jax.ShapeDtypeStruct((NB * (SX - 2) * SY, 256), BF16),
            jax.ShapeDtypeStruct((4 * EX, LANES), F32),
        ),
        in_specs=[pl.BlockSpec(memory_space=pl.ANY)] + [VMEM] * 6,
        out_specs=(VMEM,) * 7,
        scratch_shapes=[pltpu.VMEM((SX * SY, WIDE), BF16)] * 3,
        compiler_params=params(),
        cost_estimate=pl.CostEstimate(flops=10**8, bytes_accessed=8 * 2**20, transcendentals=0),
        name="before",
    )(begun, v, labels, lists, home, w1t, w2t)


def choose(flag, yes, no):
    return jnp.where(flag, yes.astype(F32), no.astype(F32)).astype(BF16)


def choose_columns(flag, yes, no):
    both = jnp.where(flag, yes.astype(F32), no.astype(F32))
    zero = jnp.zeros((16 - EX, LANES), F32)
    return jnp.concatenate([both[:EX], zero, both[EX:], zero], axis=0).astype(BF16)


def columns_kernel(where, mine, xb, xa, near, far):
    x_even = where[0] % 2 == 0
    y_even = where[1] % 2 == 0
    sides = jnp.concatenate([xa[...], xb[...]], axis=0).reshape(4 * SY, LANES)
    c, x, y = column_of(iota((4 * EX, 4 * SY), 0))
    k = jnp.where(x < 2, x, jnp.where((x >= EX - 2) & (x < EX), x - SX, -1))
    k = jnp.where(x_even, jnp.where(k >= 2, k - 2, jnp.where(k >= 0, k + 2, -1)), k)
    pick = ((k * SY + y == iota((4 * EX, 4 * SY), 1)) & (k >= 0)).astype(F32).astype(BF16)
    cols = (mine[...] + dot(pick, sides)).astype(BF16)

    @pl.when(y_even)
    def _():
        near[...] = cols[2 * EX :]
        far[...] = cols[: 2 * EX]

    @pl.when(jnp.logical_not(y_even))
    def _():
        near[...] = cols[: 2 * EX]
        far[...] = cols[2 * EX :]


def columns(where, mine, xb, xa):
    shape = jax.ShapeDtypeStruct((2 * EX, LANES), BF16)
    return pl.pallas_call(
        columns_kernel,
        out_shape=(shape, shape),
        in_specs=[SMEM, VMEM, VMEM, VMEM],
        out_specs=(VMEM, VMEM),
        compiler_params=params(),
        name="columns",
    )(where, mine, xb, xa)


def slabs_kernel(where, v, xa, xb, core, near, far, wb, a0, a1, a2, own, cols, raw, s0, s1, s2):
    gx, last_x = where[0], where[2] - 1
    x_even, y_even = where[0] % 2 == 0, where[1] % 2 == 0
    a, b = xa[...], xb[...]
    block = jnp.concatenate(
        [choose(x_even, b, a), v[0:2], v[SX - 2 : SX], choose(x_even, a, b)], axis=0
    ).reshape(8 * SY, LANES)
    s0[...], s1[...], s2[...] = shifts_y(widen(relu(block)))
    conv = convolve((s0, s1, s2), (0, 4 * SY), 2 * SY, wb, 2)
    residual = jnp.concatenate([block[SY : 3 * SY], block[5 * SY : 7 * SY]], axis=0)
    x = iota((NB * 4 * SY, 256), 0) // SY % 4
    inside = ((x > 0) | (gx > 0)) & ((x < 3) | (gx < last_x))
    sides = jnp.where(inside, conv + blocks(residual).astype(F32), 0.0).astype(BF16)
    sides = unblocks(sides)
    main = jnp.concatenate([sides[0 : 2 * SY], unblocks(core[...]), sides[2 * SY :]], axis=0)
    own[...] = main[SY : SY + SX * SY]
    a0[...], a1[...], a2[...] = shifts_y(widen(relu(main)))
    low = choose_columns(y_even, far[...], near[...])
    high = choose_columns(y_even, near[...], far[...])
    side = jnp.concatenate([low, high], axis=0)
    raw[...] = side
    side = relu(side)
    store_rolled(cols, widen(side))


def store_rolled(ref, wide):
    n = wide.shape[0]
    ref[0] = wide
    for kx in (1, 2):
        ref[kx] = pltpu.roll(wide, n - kx, 0)


def slabs(where, v, xa, xb, core, near, far, wb):
    full = jax.ShapeDtypeStruct((FX * SY, WIDE), BF16)
    return pl.pallas_call(
        slabs_kernel,
        out_shape=(
            full,
            full,
            full,
            jax.ShapeDtypeStruct((SX * SY, LANES), BF16),
            jax.ShapeDtypeStruct((3, 64, WIDE), BF16),
            jax.ShapeDtypeStruct((64, LANES), BF16),
        ),
        in_specs=[SMEM] + [VMEM] * 7,
        out_specs=(VMEM,) * 6,
        scratch_shapes=[pltpu.VMEM((8 * SY, WIDE), BF16)] * 3,
        compiler_params=params(),
        cost_estimate=pl.CostEstimate(flops=2 * 10**9, bytes_accessed=2**20, transcendentals=0),
        name="slabs",
    )(where, v, xa, xb, core, near, far, wb)


def outer_kernel(
    where, a0i, a1i, a2i, owni, cols, raw, ya, yb, wb1, a0, a1, a2, own, halo
):
    gx, gy = where[0], where[1]
    last_x, last_y = where[2] - 1, where[3] - 1
    y_even = gy % 2 == 0
    low = choose_columns(y_even, yb[...], ya[...])
    high = choose_columns(y_even, ya[...], yb[...])
    store_rolled(halo, widen(relu(jnp.concatenate([low, high], axis=0))))
    at = [(halo, 0), (halo, 16), (cols, 0), (cols, 16), (cols, 32), (cols, 48), (halo, 32), (halo, 48)]

    def group(g, kx, b):
        ref, start = at[g]
        return ref[kx, start : start + 16, 256 * b : 256 * b + 384]

    left = jnp.concatenate(
        [
            jnp.concatenate(
                [group(g + ky, kx, b) for ky in range(3) for kx in range(3)], axis=1
            )
            for b in range(NB)
            for g in (0, 1, 4, 5)
        ],
        axis=0,
    )
    conv = dot(left, wb1[...])
    residual = jnp.concatenate([low[16:32], raw[0:16], raw[48:64], high[0:16]], axis=0)
    residual = pltpu.roll(residual, 63, 0)
    row = iota((NB * 64, 256), 0)
    x = row % 16
    g = row // 16 % 4
    inside = ((x > 0) | (gx > 0)) & ((x < FX - 1) | (gx < last_x))
    inside = inside & ((g > 0) | (gy > 0)) & ((g < 3) | (gy < last_y))
    edge = jnp.where(inside, conv + blocks(residual).astype(F32), 0.0).astype(BF16)
    edge = unblocks(edge)
    wide = widen(relu(edge))
    for x in range(FX):
        s = SY * x
        a0[s : s + 1] = wide[x : x + 1]
        a0[s + 1 : s + 2] = wide[16 + x : 17 + x]
        a1[s : s + 1] = wide[16 + x : 17 + x]
        a1[s + SY - 1 : s + SY] = wide[32 + x : 33 + x]
        a2[s + SY - 2 : s + SY - 1] = wide[32 + x : 33 + x]
        a2[s + SY - 1 : s + SY] = wide[48 + x : 49 + x]
    for x in range(SX):
        s = SY * x
        own[s : s + 1] = edge[17 + x : 18 + x]
        own[s + SY - 1 : s + SY] = edge[33 + x : 34 + x]


def outer(where, a0, a1, a2, own, cols, raw, ya, yb, wb1, wb2, member, place, meta):
    full = jax.ShapeDtypeStruct(a0.shape, BF16)
    a0, a1, a2, own = pl.pallas_call(
        outer_kernel,
        out_shape=(full, full, full, jax.ShapeDtypeStruct(own.shape, BF16)),
        in_specs=[SMEM] + [VMEM] * 9,
        out_specs=(VMEM,) * 4,
        scratch_shapes=[pltpu.VMEM((3, 64, WIDE), BF16)],
        input_output_aliases={1: 0, 2: 1, 3: 2, 4: 3},
        compiler_params=params(),
        name="outer",
    )(where, a0, a1, a2, own, cols, raw, ya, yb, wb1)
    return pl.pallas_call(
        second_kernel,
        out_shape=jax.ShapeDtypeStruct((place.shape[0], 128), BF16),
        in_specs=[VMEM] * 8,
        out_specs=VMEM,
        scratch_shapes=[pltpu.VMEM((256 * NB, 128), BF16)],
        compiler_params=params(),
        name="second",
    )(a0, a1, a2, own, wb2, member, place, meta)


def second_kernel(a0, a1, a2, own, wb2, member, place, meta, out, fresh):
    slots = meta.shape[0]
    for b in range(NB):
        at = 256 * b
        left = jnp.concatenate(
            [
                ref[kx * SY : kx * SY + SX * SY, at : at + 384]
                for ref in (a0, a1, a2)
                for kx in range(3)
            ],
            axis=1,
        )
        second = dot(left, wb2[...]) + own[:, at : at + 256].astype(F32)
        fresh[at : at + 128] = second[:, 0:128].astype(BF16)
        fresh[at + 128 : at + 256] = second[:, 128:256].astype(BF16)
    odd = dot(member[slots : 2 * slots], fresh[...])
    even = dot(member[0:slots], fresh[...])
    lanes = iota((slots, 128), 1)
    sums = even + pltpu.roll(odd, 64, 1)
    rows = jnp.where(lanes < CH, sums, meta[...].astype(F32)).astype(BF16)
    step = place.shape[0] // 4
    for k in range(4):
        at = k * step
        out[at : at + step] = dot(place[at : at + step], rows).astype(BF16)


def head_kernel(got, w_in, w_out, out):
    rows = got[...]
    n = rows.shape[0]
    seg = out.shape[0]
    unit = (iota((8, 128), 1) == CH).astype(F32).astype(BF16)
    key = lax.dot_general(unit, rows, (((1,), (1,)), ((), ())), preferred_element_type=F32)
    key = jnp.broadcast_to(key[0:1], (seg, n))
    hit = (key == (iota((seg, n), 0) + 1).astype(F32)).astype(F32).astype(BF16)
    total = dot(hit, rows)
    lanes = iota((seg, 128), 1)
    digits = jnp.where(lanes == CH + 1, total * 64.0, jnp.where(lanes == CH + 2, total, 0.0))
    count = jnp.sum(digits, axis=1, keepdims=True)
    means = (total[:, 0:CH] / jnp.maximum(count, 1.0)).astype(BF16)
    hidden = jnp.maximum(dot(means, w_in[...]), 0.0).astype(BF16)
    out[...] = dot(hidden, w_out[...]).astype(BF16)


def head(got, w_in, w_out, seg):
    return pl.pallas_call(
        head_kernel,
        out_shape=jax.ShapeDtypeStruct((seg, w_out.shape[1]), BF16),
        in_specs=[VMEM] * 3,
        out_specs=VMEM,
        compiler_params=params(),
        name="head",
    )(got, w_in, w_out)


def pairs(count):
    inner_pairs = [(i, i ^ 1) for i in range(count)]
    outer_pairs = [(i, i + 1 if i % 2 else i - 1) for i in range(1, count - 1)]
    return inner_pairs, outer_pairs


def local(n_gx, n_gy, features, labels, lists, home, conv_first, conv_second, head_in, head_out):
    gx = lax.axis_index("gx")
    gy = lax.axis_index("gy")
    devices = n_gx * n_gy
    where = jnp.stack([gx, gy, jnp.int32(n_gx), jnp.int32(n_gy)]).astype(jnp.int32)
    even = gx % 2 == 0
    to_a = lax.dynamic_slice_in_dim(features, jnp.where(even, SX - 2, 0), 2, 0)
    to_b = lax.dynamic_slice_in_dim(features, jnp.where(even, 0, SX - 2), 2, 0)
    inner_x, outer_x = pairs(n_gx)
    inner_y, outer_y = pairs(n_gy)
    xb = lax.ppermute(to_b, "gx", outer_x)
    xa = lax.ppermute(to_a, "gx", inner_x)
    wb1, wb2, member, place, meta, core, mine = before(
        begin(), features, labels, lists, home.reshape(-1, 128), conv_first.T, conv_second.T, devices
    )
    near, far = columns(where, mine, xb, xa)
    yb = lax.ppermute(far, "gy", outer_y)
    ya = lax.ppermute(near, "gy", inner_y)
    a0, a1, a2, own, cols, raw = slabs(where, features, xa, xb, core, near, far, wb1)
    rows = outer(where, a0, a1, a2, own, cols, raw, ya, yb, wb1, wb2, member, place, meta)
    rows = rows.reshape(devices, CAP, 128)
    got = lax.all_to_all(rows, ("gx", "gy"), 0, 0, tiled=True)
    return head(got.reshape(devices * CAP, 128), head_in, head_out, home.size // devices)


def solution(mesh):
    placed = (
        P("gx", "gy", None),
        P("gx", "gy", None),
        P(("gx", "gy"), None),
        P(),
        P(),
        P(),
        P(),
        P(),
    )
    return jax.shard_map(
        functools.partial(local, mesh.shape["gx"], mesh.shape["gy"]),
        mesh=mesh,
        in_specs=placed,
        out_specs=P(("gx", "gy"), None),
        check_vma=False,
    )
```
